128 devices in a mesh: sec: 2 (over x_hi), oy: 8 (over z, core), ox: 8 (over x_lo, y).
Axes of the slice: x: 4 (x_hi: 2, x_lo: 2; x = x_hi * 2 + x_lo), y: 4, z: 4, core: 2. Of those that a mesh axis runs over, the one named last changes fastest.
Arguments:
- tracers: float32 [8, 62, 64, 2048], P('sec', None, 'oy', 'ox'), may hold values from -6 to 6
- zonal_velocity: float32 [62, 64, 2048], P(None, 'oy', 'ox'), may hold values from -0.12 to 0.12
- meridional_velocity: float32 [62, 64, 2048], P(None, 'oy', 'ox'), may hold values from -0.12 to 0.12
- diffusivity: float32 [62, 64, 2048], P(None, 'oy', 'ox'), may hold values from 0.01 to 0.12
- land_sea: int32 [64, 2048], P('oy', 'ox'), may hold values 0 or 1
- mix_class: int32 [64, 2048], P('oy', 'ox'), may hold values from 0 to 7
- mix_matrices: float32 [8, 62, 62], replicated, may hold values from 0 to 1
- atmos_fluxes: bfloat16 [8, 512, 1024], P(None, ('sec', 'oy'), 'ox'), may hold values from -6 to 6
- remap_weights: bfloat16 [8, 512, 4, 128, 128], P('ox', ('sec', 'oy')), may hold values from -0.1875 to 0.1875
- dest_tiles: int32 [8, 512, 4], replicated, may hold values from 0 to 127, all different within a row; in each aligned block of 32 rows (0 to 31, 32 to 63, ..., all dimensions but the last counted through in order) at most 2 rows name the same one
- dest_offsets: int32 [8, 512, 4], replicated, may hold values from 0 to 7
Outputs:
- new_tracers: float32 [8, 62, 64, 2048], P('sec', None, 'oy', 'ox')
- surface_flux: float32 [8, 64, 2048], P(None, 'oy', 'ox')
The draws below stay inside these ranges and needn't reach their ends.
Inputs may be any that keep to these rules, and one draw needn't show every extreme that they name: `dest_tiles`: each atmosphere block names 4 different devices; among the rows of one device no device is named by more than 2 blocks, and some device by exactly 2.
All inputs are finite; a program needn't handle non-finite values. No bound on the sum of `land_sea` on one device may be relied on, other than what follows from the above.
Results may differ from the reference program's by a relative error of at most 0.0003.
Values sent between devices are 32-bit elements; how exact they have to be, the bound alone decides.
No kernel may reach another device: no remote copies, remote signals or barrier semaphores. Data moves between devices by JAX's collectives and lax.ppermute only.
A program may use at most 128 MiB of HBM per device.

```python
import math
import jax
import jax.numpy as jnp
import numpy as np
from jax import lax

NFLUX = 8
TRACERS = 8
LEV = 62
MIXK = 8
OBC = 128
ABC = 128
NDST = 4
SUBSTEPS = 2
AR_DEV = 32
OY_DEV = 8
HALF = 4
NBR = 2
NBO = 8
NY = 64
NX = 2048
AROWS = 512
ACOLS = 1024
CAP = 2
N_OY = 8
N_OX = 8
DEVICES = 128


def draw_mix_matrices(key, part):
    key = jax.random.fold_in(key, 11)
    key_length, key_rough = jax.random.split(key)
    length = jnp.exp(jax.random.uniform(key_length, (MIXK, 1, 1), jnp.float32, math.log(3.0), math.log(40.0)))
    rough_part = jax.random.uniform(key_rough, (MIXK, LEV, LEV), jnp.float32, 0.5, 1.5)
    level_row = jnp.arange(LEV, dtype=jnp.float32)[:, None]
    level_col = jnp.arange(LEV, dtype=jnp.float32)[None, :]
    distance = jnp.abs(level_row - level_col)[None]
    identity = jnp.where(distance == 0.0, 1.0, 0.0)
    spread = 0.5 * rough_part * jnp.exp(-distance / length) / (2.0 * length + 1.0)
    return (0.5 * identity + spread).astype(jnp.float32)


def touch_ends(drawn, stream_key, least, top_value):
    place = [jax.random.randint(jax.random.fold_in(stream_key, axis), (), 0, length) for axis, length in enumerate(drawn.shape)]
    longest = drawn.shape.index(max(drawn.shape))
    neighbour = place[:longest] + [(place[longest] + 1) % drawn.shape[longest]] + place[longest + 1:]
    return drawn.at[tuple(place)].set(least).at[tuple(neighbour)].set(top_value)


def block_levels(key, dims, pieces, least, high):
    factor_of = 1.0
    for axis_at, shards_of in pieces:
        draws = jax.random.uniform(jax.random.fold_in(jax.random.fold_in(key, 6), axis_at), (shards_of,), jnp.float32, least / len(pieces), high / len(pieces))
        factor_of = factor_of * jnp.repeat(jnp.exp(draws), dims[axis_at] // shards_of).reshape((-1,) + (1,) * (len(dims) - 1 - axis_at))
    return factor_of


def shared_out(stream_key, own, number, rows, count, top, bound, skew):
    order = jax.random.permutation(stream_key, count)
    crowded, ordinary = load_shares(count, rows * top, bound, skew, True), load_shares(count, rows * top, bound, skew, False)
    places = jnp.arange(count)

    def named(tallies, turn):
        used = int((tallies > 0).sum())
        fixed = max(1, used // 4)
        passed = fixed + (places - fixed + turn * (used - fixed)) % max(1, count - fixed)
        return jnp.zeros((count,), jnp.int32).at[order[jnp.where(places < fixed, places, passed)]].set(jnp.asarray(tallies, jnp.int32))

    tallies = jnp.where(number % 4 == 0, named(crowded, number // 4), named(ordinary, number - number // 4 - 1))
    mixed = jax.random.permutation(jax.random.fold_in(own, 3), count)
    source_of, sink = mixed[0:count // 2 * 2:2], mixed[1:count // 2 * 2:2]
    margin = jnp.minimum(tallies[source_of] - 1, bound - tallies[sink]) // 2
    margin = jnp.where((source_of == order[0]) | (sink == order[0]) | (tallies[sink] == 0), 0, jnp.maximum(margin, 0))
    passed = jax.random.randint(jax.random.fold_in(own, 4), (count // 2,), 0, 1 << 20) % (margin + 1)
    tallies = tallies.at[source_of].add(-passed).at[sink].add(passed)
    members = jnp.searchsorted(jnp.cumsum(tallies), jnp.arange(rows * top), side="right").astype(jnp.int32)
    grid = members.reshape(top, rows).T
    grid = grid[jax.random.permutation(jax.random.fold_in(own, 1), rows)]
    turn = jax.random.randint(jax.random.fold_in(own, 2), (rows, 1), 0, top)
    return jnp.take_along_axis(grid, (jnp.arange(top)[None, :] + turn) % top, axis=1)


def load_shares(count, total, limit, slope, full):
    loads = [(1 << 20) // math.isqrt(standing ** slope) + 1 for standing in range(1, count + 1)]
    largest = limit if full else min(limit, max(-(-total // count), total * loads[0] // sum(loads)))
    least = 1 if total - largest >= count - 1 else 0
    given, surplus = [largest] + [least] * (count - 1), total - largest - least * (count - 1)
    while surplus > 0:
        candidates = [i for i in range(1, count) if given[i] < largest] or [i for i in range(1, count) if given[i] < limit]
        pool, remaining = sum([loads[i] for i in candidates]), surplus
        for i in candidates:
            addition = min(limit - given[i], max(1, remaining * loads[i] // pool), surplus)
            given[i] = given[i] + addition
            surplus = surplus - addition
    return np.array(given)


def noise(own_key, extent, scale, bound, cuts=(), kind=jnp.bfloat16):
    values = scale * jax.random.normal(own_key, extent, jnp.float32)
    if cuts:
        values = values * block_levels(own_key, extent, cuts, -0.22, 0.18)
    return jnp.clip(values, -bound, bound).astype(kind)


def setup_inputs(seed: int = 0) -> dict:
    seeds = jax.random.split(jax.random.key(seed), 12)
    tracers = noise(seeds[0], (TRACERS, LEV, NY, NX), 1.0, 6.0, ((0, 2), (2, 8), (3, 8)), jnp.float32)
    zonal_velocity = jnp.clip(jax.random.uniform(seeds[1], (LEV, NY, NX), jnp.float32, -0.12, 0.12) * block_levels(seeds[1], (LEV, NY, NX), ((1, 8), (2, 8)), -0.4, 0.0), -0.12, 0.12)
    meridional_velocity = jnp.clip(jax.random.uniform(seeds[2], (LEV, NY, NX), jnp.float32, -0.12, 0.12) * block_levels(seeds[2], (LEV, NY, NX), ((1, 8), (2, 8)), -0.4, 0.0), -0.12, 0.12)
    diffusivity = jnp.clip(jnp.exp(math.log(0.12) - 2.4849066 * jax.random.uniform(seeds[3], (LEV, NY, NX), jnp.float32) ** block_levels(seeds[3], (LEV, NY, NX), ((1, 8), (2, 8)), -0.2, 0.2)), 0.01, 0.12)
    land_sea = touch_ends((jax.random.randint(seeds[4], (NY, NX), 0, 8) < 7).astype(jnp.int32), jax.random.fold_in(seeds[4], 1), 0, 1)
    mix_class = touch_ends(jax.random.randint(seeds[5], (NY, NX), 0, MIXK), jax.random.fold_in(seeds[5], 1), 0, MIXK - 1).astype(jnp.int32)
    mix_matrices = draw_mix_matrices(jax.random.fold_in(seeds[11], 71), 0)
    atmos_fluxes = noise(seeds[7], (NFLUX, AROWS, ACOLS), 1.0, 6.0, ((1, 16), (2, 8)))
    remap_weights = noise(seeds[8], (N_OX, AROWS, NDST, ABC, OBC), (ABC * 8) ** -0.5, 0.1875, ((0, 8), (1, 16)))
    dest_tiles_keys = jax.random.split(jax.random.fold_in(seeds[9], 1), N_OX * AROWS // AR_DEV)
    dest_tiles_turns = jax.random.permutation(jax.random.fold_in(seeds[9], 3), N_OX * AROWS // AR_DEV)
    dest_tiles = jax.vmap(lambda own, number: shared_out(jax.random.fold_in(seeds[9], 2), own, number, AR_DEV, DEVICES, NDST, CAP, 1))(dest_tiles_keys, dest_tiles_turns).reshape((N_OX, AROWS, NDST))
    dest_offsets = touch_ends(jax.random.randint(seeds[10], (N_OX, AROWS, NDST), 0, NBO), jax.random.fold_in(seeds[10], 1), 0, NBO - 1).astype(jnp.int32)
    return {"tracers": tracers, "zonal_velocity": zonal_velocity, "meridional_velocity": meridional_velocity, "diffusivity": diffusivity, "land_sea": land_sea, "mix_class": mix_class, "mix_matrices": mix_matrices, "atmos_fluxes": atmos_fluxes, "remap_weights": remap_weights, "dest_tiles": dest_tiles, "dest_offsets": dest_offsets}


def pad_rims(array):
    widths = [(0, 0)] * (array.ndim - 2) + [(1, 1), (0, 0)]
    padded = jnp.pad(array, widths)
    return jnp.concatenate([padded[..., -1:], padded, padded[..., :1]], axis=-1)


def transport(padded, zonal_pad, merid_pad, diff_pad, wet_pad):
    center = padded[:, :, 1:-1, 1:-1]
    west_cell = padded[:, :, 1:-1, :-1]
    east_cell = padded[:, :, 1:-1, 1:]
    east_vel = 0.5 * (zonal_pad[:, 1:-1, :-1] + zonal_pad[:, 1:-1, 1:])
    east_dif = 0.5 * (diff_pad[:, 1:-1, :-1] + diff_pad[:, 1:-1, 1:])
    east_wet = wet_pad[1:-1, :-1] * wet_pad[1:-1, 1:]
    east_flux = east_wet * (jnp.maximum(east_vel, 0.0) * west_cell + jnp.minimum(east_vel, 0.0) * east_cell - east_dif * (east_cell - west_cell))
    south_cell = padded[:, :, :-1, 1:-1]
    north_cell = padded[:, :, 1:, 1:-1]
    north_vel = 0.5 * (merid_pad[:, :-1, 1:-1] + merid_pad[:, 1:, 1:-1])
    north_dif = 0.5 * (diff_pad[:, :-1, 1:-1] + diff_pad[:, 1:, 1:-1])
    north_wet = wet_pad[:-1, 1:-1] * wet_pad[1:, 1:-1]
    north_flux = north_wet * (jnp.maximum(north_vel, 0.0) * south_cell + jnp.minimum(north_vel, 0.0) * north_cell - north_dif * (north_cell - south_cell))
    return center - (east_flux[..., 1:] - east_flux[..., :-1] + north_flux[..., 1:, :] - north_flux[..., :-1, :])


def surface_forcing(tracer_field, flux_field, wet_cells, heat_select):
    heat_flux = flux_field[0] + flux_field[1] + flux_field[2] + flux_field[3]
    fresh_flux = flux_field[5] - flux_field[4]
    stress = 0.5 * (flux_field[6] * flux_field[6] + flux_field[7] * flux_field[7])
    select = heat_select[:, None, None]
    top_level = tracer_field[:, 0]
    top_level = top_level + wet_cells * (0.25 * select * heat_flux + 0.1 * (1.0 - select) * fresh_flux * top_level)
    second = tracer_field[:, 1]
    weight = wet_cells * 0.5 * stress / (1.0 + stress)
    new_top = top_level + weight * (second - top_level)
    new_second = second + weight * (top_level - second)
    return jnp.concatenate([new_top[:, None], new_second[:, None], tracer_field[:, 2:]], axis=1)


def column_mixing(tracer_field, mix_class, mix_matrices):
    full_shape = tracer_field.shape
    columns = tracer_field.reshape(full_shape[0], full_shape[1], -1)
    class_flat = mix_class.reshape(-1)
    mixed_sum = jnp.zeros_like(columns)
    for class_id in range(mix_matrices.shape[0]):
        mixed_cols = jnp.einsum('lm,nmc->nlc', mix_matrices[class_id], columns, precision=lax.Precision.HIGHEST)
        mixed_sum = mixed_sum + jnp.where(class_flat == class_id, mixed_cols, 0.0)
    return mixed_sum.reshape(full_shape)


def remap_fluxes(atmos_fluxes, remap_weights, dest_tiles, dest_offsets):
    fluxes_split = atmos_fluxes.reshape(NFLUX, AROWS, N_OX, ABC).transpose(2, 0, 1, 3)

    def one_column(inputs):
        block_flux, block_weight = inputs
        return jnp.einsum('fac,ajco->ajfo', block_flux.astype(jnp.float32), block_weight.astype(jnp.float32))

    partials = lax.map(one_column, (fluxes_split, remap_weights))
    dest = dest_tiles.astype(jnp.int32)
    offset = dest_offsets.astype(jnp.int32)
    sec_part = dest // (N_OY * N_OX)
    lat_part = (dest // N_OX) % N_OY
    lon_part = dest % N_OX
    row_of = lat_part * OY_DEV + sec_part * HALF + offset // NBR
    col_of = lon_part * NBR + offset % NBR
    segment = (row_of * (NX // OBC) + col_of).reshape(-1)
    summed = jax.ops.segment_sum(partials.reshape(-1, NFLUX * OBC), segment, num_segments=NY * (NX // OBC))
    return summed.reshape(NY, NX // OBC, NFLUX, OBC).transpose(2, 0, 1, 3).reshape(NFLUX, NY, NX)


def reference(tracers, zonal_velocity, meridional_velocity, diffusivity, land_sea, mix_class, mix_matrices, atmos_fluxes, remap_weights, dest_tiles, dest_offsets):
    surface_flux = remap_fluxes(atmos_fluxes, remap_weights, dest_tiles, dest_offsets)
    wet_cells = land_sea.astype(jnp.float32)
    zonal_pad = pad_rims(zonal_velocity)
    merid_pad = pad_rims(meridional_velocity)
    diff_pad = pad_rims(diffusivity)
    wet_pad = pad_rims(wet_cells)

    def one_tracer(inputs):
        tracer_field, tracer_id = inputs
        tracer_field = tracer_field[None]
        for substep in range(SUBSTEPS):
            tracer_field = transport(pad_rims(tracer_field), zonal_pad, merid_pad, diff_pad, wet_pad)
        heat_select = jnp.where(tracer_id == 0, 1.0, 0.0).astype(tracer_field.dtype)[None]
        tracer_field = surface_forcing(tracer_field, surface_flux, wet_cells, heat_select)
        return column_mixing(tracer_field, mix_class, mix_matrices)[0]

    new_tracers = lax.map(one_tracer, (tracers, jnp.arange(TRACERS, dtype=jnp.int32)))
    return new_tracers, surface_flux
```

```python
import jax
import jax.numpy as jnp
from jax import lax
from jax.experimental import pallas as pl
from jax.experimental.pallas import tpu as pltpu
from jax.sharding import PartitionSpec as P

F32 = jnp.float32
BF16 = jnp.bfloat16
VMEM_LIMIT = 28 * 1024 * 1024
UNROLL_ONE = 2
UNROLL_PACK = True
UNROLL_TWO = True
UNROLL_MIX = 4
VM = pl.BlockSpec(memory_space=pltpu.VMEM)
SM = pl.BlockSpec(memory_space=pltpu.SMEM)
OY, OX, SEC, N_OY = 0, 1, 2, 3


def call(body, outs, in_specs, scratch=(), **kw):
    if all(spec.block_shape is None for spec in in_specs):
        return pl.pallas_call(
            body,
            out_shape=outs,
            in_specs=in_specs,
            out_specs=jax.tree.map(lambda _: VM, outs),
            scratch_shapes=list(scratch),
            compiler_params=pltpu.CompilerParams(vmem_limit_bytes=VMEM_LIMIT),
            **kw,
        )
    return pl.pallas_call(
        body,
        out_shape=outs,
        grid=(1,),
        in_specs=in_specs,
        out_specs=jax.tree.map(lambda _: VM, outs),
        scratch_shapes=list(scratch),
        compiler_params=pltpu.CompilerParams(vmem_limit_bytes=VMEM_LIMIT),
        **kw,
    )


def shape(*dims, dtype=F32):
    return jax.ShapeDtypeStruct(dims, dtype)


def lanes(*halves):
    return jnp.concatenate(halves, axis=1)


def load(halves, at, n=8, stride=None):
    return lanes(*(half[pl.ds(at, n, stride=stride), :] for half in halves))


def store(halves, value, at, n=8, stride=None):
    for h, half in enumerate(halves):
        half[pl.ds(at, n, stride=stride), :] = value[:, h * 128 : h * 128 + 128]


def pair(ref):
    return ref.at[0], ref.at[1]


def half_specs(rows):
    return [pl.BlockSpec((rows, 128), lambda _, h=h: (0, h)) for h in range(2)]


def remap_kernel(own_ref, flux_ref, weight_ref, out_ref, rows_ref, count_ref):
    step = pl.program_id(0)
    block_rows = weight_ref.shape[0]
    fluxes, atm_rows, cells = flux_ref.shape
    dests = weight_ref.shape[1]
    half = out_ref.shape[0] // 4

    @pl.when(step == 0)
    def _():
        out_ref[...] = jnp.zeros_like(out_ref)
        rows_ref[...] = flux_ref[...].astype(F32).reshape(fluxes * atm_rows, cells)

        def clear(i, _):
            count_ref[i] = 0
            return 0

        lax.fori_loop(0, 2 * half, clear, 0, unroll=8)

    for i in range(block_rows):
        row = step * block_rows + i
        lhs = rows_ref[pl.ds(row, fluxes, stride=atm_rows), :].astype(BF16)
        for j in range(dests):
            part = jnp.dot(lhs, weight_ref[i, j], preferred_element_type=F32)
            dest = own_ref[j, row]
            rank = count_ref[dest]
            count_ref[dest] = rank + 1
            upper = (dest >= half).astype(jnp.int32)
            slot = (dest - upper * half) * 4 + upper * 2 + jnp.minimum(rank, 1)
            out_ref[slot] = part


def remap(own, atmos_fluxes, weights, pools):
    fluxes, atm_rows, cells = atmos_fluxes.shape
    dests, _, out_cells = weights.shape[1:]
    steps = 8
    block = atm_rows // steps
    return pl.pallas_call(
        remap_kernel,
        out_shape=shape(pools * 4, fluxes, out_cells),
        grid=(steps,),
        in_specs=[
            SM,
            pl.BlockSpec((fluxes, atm_rows, cells), lambda i: (0, 0, 0)),
            pl.BlockSpec((block, dests, cells, out_cells), lambda i: (i, 0, 0, 0)),
        ],
        out_specs=pl.BlockSpec((pools * 4, fluxes, out_cells), lambda i: (0, 0, 0)),
        scratch_shapes=[
            pltpu.VMEM((fluxes * atm_rows, cells), F32),
            pltpu.SMEM((2 * pools,), jnp.int32),
        ],
        compiler_params=pltpu.CompilerParams(vmem_limit_bytes=VMEM_LIMIT),
    )(own, atmos_fluxes, weights)


def table_kernel(sc_ref, dest_ref, offset_ref, out_ref):
    sources, parts = dest_ref.shape
    pool = sc_ref[OY] * (sources // sc_ref[N_OY]) + sc_ref[OX]
    dest = dest_ref[...]
    offset = offset_ref[...]
    before = (
        lax.broadcasted_iota(jnp.int32, (parts, parts), 0)
        < lax.broadcasted_iota(jnp.int32, (parts, parts), 1)
    ).astype(F32).astype(BF16)
    lane = lax.broadcasted_iota(jnp.int32, (sources, 128), 1)
    columns = []
    for s in range(2):
        hit = dest == pool + s * sources
        rank = jnp.dot(
            jnp.where(hit, 1.0, 0.0).astype(BF16), before, preferred_element_type=F32
        )
        place = (offset & 1) * 8 + s * 4 + (offset >> 1) + 1
        for r in range(2):
            chosen = hit & (rank == float(r))
            where_to = jnp.sum(jnp.where(chosen, place, 0).astype(F32), axis=1, keepdims=True)
            columns.append(jnp.where(where_to == (lane + 1).astype(F32), 1.0, 0.0))
    onehot = jnp.concatenate(columns, axis=0)
    out_ref[...] = jnp.transpose(onehot)[:16]


def combine_kernel(onehot_ref, recv_ref, out_ref):
    fluxes = out_ref.shape[0]
    slots = onehot_ref.shape[1]
    sources = slots // 4
    onehot = onehot_ref[...].astype(BF16)
    for f in range(fluxes):
        cells = jnp.concatenate(
            [recv_ref[pl.ds(n * fluxes + f, sources, stride=4 * fluxes), :] for n in range(4)],
            axis=0,
        )
        high = cells.astype(BF16)
        rest = cells - high.astype(F32)
        mid = rest.astype(BF16)
        low = (rest - mid.astype(F32)).astype(BF16)
        both = jnp.dot(
            onehot, jnp.concatenate([high, mid], axis=1), preferred_element_type=F32
        )
        total = both[:, :128] + (
            both[:, 128:] + jnp.dot(onehot, low, preferred_element_type=F32)
        )
        out_ref[f, :, :128] = total[:8]
        out_ref[f, :, 128:] = total[8:]


def pack_columns(first, last, level, acc_west, acc_east):
    lane = lax.broadcasted_iota(jnp.int32, first.shape, 1)
    west = jnp.where(lane == level, pltpu.roll(first, level, 1), acc_west)
    east = jnp.where(lane == level, pltpu.roll(last, level + 1, 1), acc_east)
    return west, east


def pack_fields(fields, levels):
    zero = jnp.zeros((8, 128), F32)

    def body(level, accs):
        new = []
        for (ref, base), (acc_west, acc_east) in zip(fields, accs):
            at = pl.multiple_of((base + level) * 8, 8)
            first, last = (half[pl.ds(at, 8), :] for half in ref)
            new.append(pack_columns(first, last, level, acc_west, acc_east))
        return tuple(new)

    return lax.fori_loop(0, levels, body, tuple((zero, zero) for _ in fields), unroll=UNROLL_PACK)


def pack_kernel(
    sc_ref, tr0, tr1, u0, u1, v0, v1, k0, k1, land_ref, nsa_ref, nsb_ref, ewa_ref, ewb_ref
):
    tr_ref, u_ref, v_ref, k_ref = (tr0, tr1), (u0, u1), (v0, v1), (k0, k1)
    levels = u0.shape[0] // 8
    tracers = tr0.shape[0] // u0.shape[0]
    even_y = sc_ref[OY] % 2 == 0
    even_x = sc_ref[OX] % 2 == 0
    wet = land_ref[...].astype(F32)
    count = tracers * levels
    v_at = count
    k_at = count + 64
    w_at = count + 128

    def rows(ref, n, at):
        north = load(ref, 7, n, 8)
        south = load(ref, 0, n, 8)
        nsa_ref[at : at + n, :] = jnp.where(even_y, north, south)
        nsb_ref[at : at + n, :] = jnp.where(even_y, south, north)

    rows(tr_ref, count, 0)
    rows(v_ref, levels, v_at)
    rows(k_ref, levels, k_at)
    north = jnp.broadcast_to(wet[7:8], wet.shape)
    south = jnp.broadcast_to(wet[0:1], wet.shape)
    nsa_ref[w_at : w_at + 8, :] = jnp.where(even_y, north, south)
    nsb_ref[w_at : w_at + 8, :] = jnp.where(even_y, south, north)
    nsa_ref[v_at + levels : k_at, :] = jnp.zeros((64 - levels, 256), F32)
    nsb_ref[v_at + levels : k_at, :] = jnp.zeros((64 - levels, 256), F32)
    nsa_ref[k_at + levels : w_at, :] = jnp.zeros((64 - levels, 256), F32)
    nsb_ref[k_at + levels : w_at, :] = jnp.zeros((64 - levels, 256), F32)

    accs = pack_fields([(tr_ref, t * levels) for t in range(tracers)] + [(u_ref, 0), (k_ref, 0)], levels)
    accs = accs + (
        (
            jnp.broadcast_to(wet[:, :1], (8, 128)),
            jnp.broadcast_to(wet[:, 255:], (8, 128)),
        ),
    )
    for n, (west, east) in enumerate(accs):
        ewa_ref[n * 8 : n * 8 + 8, :] = jnp.where(even_x, east, west)
        ewb_ref[n * 8 : n * 8 + 8, :] = jnp.where(even_x, west, east)


def face(vel_left, vel_right, dif_left, dif_right, ww):
    velocity = 0.5 * (vel_left + vel_right)
    spread = 0.5 * (dif_left + dif_right)
    return (
        ww * (jnp.maximum(velocity, 0.0) + spread),
        ww * (jnp.minimum(velocity, 0.0) - spread),
    )


def east_of(x, rim):
    lane = lax.broadcasted_iota(jnp.int32, (8, 128), 1)
    first, last = (pltpu.roll(half, 127, 1) for half in x)
    return jnp.where(lane == 127, last, first), jnp.where(lane == 127, rim, last)


def west_of(x, rim):
    lane = lax.broadcasted_iota(jnp.int32, (8, 128), 1)
    first, last = (pltpu.roll(half, 1, 1) for half in x)
    return jnp.where(lane == 0, rim, first), jnp.where(lane == 0, first, last)


def north_of(x, rim):
    row = lax.broadcasted_iota(jnp.int32, (8, 128), 0)
    return tuple(jnp.where(row == 7, r, pltpu.roll(half, 7, 0)) for half, r in zip(x, rim))


def south_of(x, rim):
    row = lax.broadcasted_iota(jnp.int32, (8, 128), 0)
    return tuple(jnp.where(row == 0, r, pltpu.roll(half, 1, 0)) for half, r in zip(x, rim))


def to_last(rim, level):
    return pltpu.roll(rim, 127 - level, 1)


def to_first(rim, level):
    return pltpu.roll(rim, (128 - level) % 128, 1)


def tile(halves, at):
    return tuple(half[pl.ds(at, 8), :] for half in halves)


def put(halves, value, at):
    for half, x in zip(halves, value):
        half[pl.ds(at, 8), :] = x


def one_row(ref, at):
    return split(ref[pl.ds(at, 1), :])


def split(x):
    return x[:, :128], x[:, 128:]


def stencil(coefs, x, east, west, north, south):
    middle, ce, cw, cn, cs = coefs
    e, w, n, s = east_of(x, east), west_of(x, west), north_of(x, north), south_of(x, south)
    return tuple(
        (middle[h] * x[h] + (ce[h] * e[h] + cw[h] * w[h])) + (cn[h] * n[h] + cs[h] * s[h])
        for h in range(2)
    )


def step_one_kernel(
    sc_ref, tr0, tr1, u0, u1, v0, v1, k0, k1, land_ref,
    nsa_ref, nsb_ref, ewa_ref, ewb_ref, sewa_ref, sewb_ref,
    new_ref, coef_ref, nsa_out, nsb_out, ewa_out, ewb_out,
    north_ref, south_ref, fn_ref, fs_ref,
):
    tr_ref, u_ref, v_ref, k_ref = (tr0, tr1), (u0, u1), (v0, v1), (k0, k1)
    new_halves = pair(new_ref)
    levels = u0.shape[0] // 8
    tracers = tr0.shape[0] // u0.shape[0]
    count = tracers * levels
    even_y = sc_ref[OY] % 2 == 0
    even_x = sc_ref[OX] % 2 == 0
    keep_north = (sc_ref[OY] < sc_ref[N_OY] - 1).astype(F32)
    keep_south = (sc_ref[OY] > 0).astype(F32)
    v_at, k_at, w_at = count, count + 64, count + 128
    a, b = nsa_ref[...], nsb_ref[...]
    north_ref[...] = jnp.where(even_y, a, b)
    south_ref[...] = jnp.where(even_y, b, a)
    a, b = ewa_ref[...], ewb_ref[...]
    east = jnp.where(even_x, a, b)
    west = jnp.where(even_x, b, a)
    a, b = sewa_ref[...], sewb_ref[...]
    own_east = jnp.where(even_x, a, b)
    own_west = jnp.where(even_x, b, a)

    wet = land_ref[...].astype(F32)
    f_a, f_b = face(
        load(v_ref, 7, levels, 8), north_ref[v_at : v_at + levels, :],
        load(k_ref, 7, levels, 8), north_ref[k_at : k_at + levels, :],
        wet[7:8] * north_ref[w_at : w_at + 1, :] * keep_north,
    )
    fn_ref[0, :levels, :] = f_a
    fn_ref[1, :levels, :] = f_b
    f_a, f_b = face(
        south_ref[v_at : v_at + levels, :], load(v_ref, 0, levels, 8),
        south_ref[k_at : k_at + levels, :], load(k_ref, 0, levels, 8),
        wet[0:1] * south_ref[w_at : w_at + 1, :] * keep_south,
    )
    fs_ref[0, :levels, :] = f_a
    fs_ref[1, :levels, :] = f_b
    n_u, n_k, n_w = 8 * tracers, 8 * (tracers + 1), 8 * (tracers + 2)
    east_a, east_b = face(
        own_east[n_u:n_k], east[n_u:n_k], own_east[n_k:n_w], east[n_k:n_w],
        own_east[n_w:] * east[n_w:],
    )
    west_a, west_b = face(
        west[n_u:n_k], own_west[n_u:n_k], west[n_k:n_w], own_west[n_k:n_w],
        own_west[n_w:] * west[n_w:],
    )

    no_rim = jnp.zeros((8, 128), F32)
    wet_halves = split(wet)
    ww_east = tuple(w * e for w, e in zip(wet_halves, east_of(wet_halves, no_rim)))
    ww_north = tuple(w * n for w, n in zip(wet_halves, north_of(wet_halves, (no_rim, no_rim))))
    last_lane = lax.broadcasted_iota(jnp.int32, (8, 128), 1) == 127
    top_row = lax.broadcasted_iota(jnp.int32, (8, 128), 0) == 7
    faces_north = fn_ref.at[0], fn_ref.at[1]
    faces_south = fs_ref.at[0], fs_ref.at[1]

    def body(level, _):
        at = pl.multiple_of(level * 8, 8)
        ul, vl, kl = tile(u_ref, at), tile(v_ref, at), tile(k_ref, at)
        ue, ke = east_of(ul, no_rim), east_of(kl, no_rim)
        vn = tuple(pltpu.roll(half, 7, 0) for half in vl)
        kn = tuple(pltpu.roll(half, 7, 0) for half in kl)
        ae, be = zip(*(face(ul[h], ue[h], kl[h], ke[h], ww_east[h]) for h in range(2)))
        an, bn = zip(*(face(vl[h], vn[h], kl[h], kn[h], ww_north[h]) for h in range(2)))
        ae = ae[0], jnp.where(last_lane, to_last(east_a, level), ae[1])
        be = be[0], jnp.where(last_lane, to_last(east_b, level), be[1])
        aw, bw = west_of(ae, to_first(west_a, level)), west_of(be, to_first(west_b, level))
        an = tuple(jnp.where(top_row, r, x) for r, x in zip(one_row(faces_north[0], level), an))
        bn = tuple(jnp.where(top_row, r, x) for r, x in zip(one_row(faces_north[1], level), bn))
        as_ = south_of(an, one_row(faces_south[0], level))
        bs = south_of(bn, one_row(faces_south[1], level))
        middle = tuple(((1.0 - ae[h]) + bw[h]) + (bs[h] - an[h]) for h in range(2))
        coefs = middle, tuple(-x for x in be), aw, tuple(-x for x in bn), as_
        for n, x in enumerate(coefs):
            put(pair(coef_ref.at[n]), x, at)
        for t in range(tracers):
            src = pl.multiple_of((t * levels + level) * 8, 8)
            rim = slice(8 * t, 8 * t + 8)
            y = stencil(
                coefs, tile(tr_ref, src), to_last(east[rim], level), to_first(west[rim], level),
                one_row(north_ref, t * levels + level), one_row(south_ref, t * levels + level),
            )
            put(new_halves, y, src)
        return 0

    lax.fori_loop(0, levels, body, 0, unroll=UNROLL_ONE)
    accs = pack_fields([(new_halves, t * levels) for t in range(tracers)], levels)
    for n, (w, e) in enumerate(accs):
        ewa_out[n * 8 : n * 8 + 8, :] = jnp.where(even_x, e, w)
        ewb_out[n * 8 : n * 8 + 8, :] = jnp.where(even_x, w, e)
    north = load(new_halves, 7, count, 8)
    south = load(new_halves, 0, count, 8)
    nsa_out[...] = jnp.where(even_y, north, south)
    nsb_out[...] = jnp.where(even_y, south, north)


def step_two_kernel(
    sc_ref, tr_ref, coef_ref, nsa_ref, nsb_ref, ewa_ref, ewb_ref, mats_ref, top_mats_ref, class_ref,
    pre_ref, unit_ref, top_ref,
    north_ref, south_ref, cells_ref, lhs_ref,
):
    levels = coef_ref.shape[2] // 8
    tracers = tr_ref.shape[1] // coef_ref.shape[2]
    moved, cells, pre = pair(tr_ref), pair(cells_ref), pair(pre_ref)
    classes = mats_ref.shape[0]
    even_y = sc_ref[OY] % 2 == 0
    even_x = sc_ref[OX] % 2 == 0
    a, b = nsa_ref[...], nsb_ref[...]
    north_ref[...] = jnp.where(even_y, a, b)
    south_ref[...] = jnp.where(even_y, b, a)
    a, b = ewa_ref[...], ewb_ref[...]
    east = jnp.where(even_x, a, b)
    west = jnp.where(even_x, b, a)

    def body(level, _):
        at = pl.multiple_of(level * 8, 8)
        coefs = [tile(pair(coef_ref.at[n]), at) for n in range(5)]
        for t in range(tracers):
            src = pl.multiple_of((t * levels + level) * 8, 8)
            rim = slice(8 * t, 8 * t + 8)
            y = stencil(
                coefs, tile(moved, src), to_last(east[rim], level), to_first(west[rim], level),
                one_row(north_ref, t * levels + level), one_row(south_ref, t * levels + level),
            )
            put(cells, y, pl.multiple_of((t * 64 + level) * 8, 8))
        return 0

    lax.fori_loop(0, levels, body, 0, unroll=UNROLL_TWO)
    for t in range(tracers):
        top_ref[t * 16 : t * 16 + 16, :] = load(cells, t * 512, 16)
        store(cells, jnp.zeros((16, 256), F32), t * 512, 16)
        store(cells, jnp.zeros((16, 256), F32), t * 512 + levels * 8, 16)

    lhs_ref[...] = jnp.zeros_like(lhs_ref)
    for k in range(classes):
        m = mats_ref[k]
        high = m.astype(BF16)
        low = (m - high.astype(F32)).astype(BF16)
        lhs_ref[k * 64 : k * 64 + levels, 0:levels] = high
        lhs_ref[k * 64 : k * 64 + levels, 64 : 64 + levels] = low
        lhs_ref[k * 64 : k * 64 + levels, 128 : 128 + levels] = high

    kinds = class_ref[...]
    top_mats = top_mats_ref[...]
    high = top_mats.astype(BF16)
    rest = top_mats - high.astype(F32)
    mid = rest.astype(BF16)
    low = (rest - mid.astype(F32)).astype(BF16)
    top_mats = jnp.concatenate([high, mid, low], axis=1)
    for lat in range(8):
        kind = kinds[lat : lat + 1, :]
        pick = jnp.where(
            lax.broadcasted_iota(jnp.int32, (classes, 256), 0) == kind, 1.0, 0.0
        )
        units = jnp.dot(
            top_mats, jnp.concatenate([pick, pick, pick], axis=0).astype(BF16),
            preferred_element_type=F32,
        )
        for n in range(2):
            store(pair(unit_ref.at[n]), units[n * 64 : n * 64 + levels], lat, levels, 8)

    def mix(n, _):
        t, lat = n // 8, n % 8
        x = load(cells, t * 512 + lat, 64, 8)
        high = x.astype(BF16)
        low = (x - high.astype(F32)).astype(BF16)
        mixed = jnp.dot(
            lhs_ref[...], jnp.concatenate([high, high, low], axis=0), preferred_element_type=F32
        )
        kind = class_ref[pl.ds(lat, 1), :]
        out = mixed[:64]
        for k in range(1, classes):
            out = jnp.where(kind == k, mixed[k * 64 : k * 64 + 64], out)
        store(pre, out[:levels], t * levels * 8 + lat, levels, 8)
        return 0

    lax.fori_loop(0, tracers * 8, mix, 0, unroll=UNROLL_MIX)


def finish_kernel(sc_ref, mine_ref, other_ref, land_ref, top_ref, unit_ref, pre_ref, out_ref, surface_ref):
    levels = unit_ref.shape[2] // 8
    tracers = pre_ref.shape[1] // unit_ref.shape[2]
    pre = pair(pre_ref)
    flux = [mine_ref[f] + other_ref[f] for f in range(8)]
    for f in range(8):
        surface_ref[f] = flux[f]
    wet = land_ref[...].astype(F32)
    heat = flux[0] + flux[1] + flux[2] + flux[3]
    fresh = flux[5] - flux[4]
    stress = 0.5 * (flux[6] * flux[6] + flux[7] * flux[7])
    weight = wet * 0.5 * stress / (1.0 + stress)
    new = []
    for t in range(tracers):
        select = ((sc_ref[SEC] == 0) & (t == 0)).astype(F32)
        top = top_ref[t * 16 : t * 16 + 8, :]
        second = top_ref[t * 16 + 8 : t * 16 + 16, :]
        top = top + wet * (0.25 * select * heat + 0.1 * (1.0 - select) * fresh * top)
        new.append((top + weight * (second - top), second + weight * (top - second)))

    def body(level, _):
        at = pl.multiple_of(level * 8, 8)
        m0, m1 = load(pair(unit_ref.at[0]), at), load(pair(unit_ref.at[1]), at)
        for t in range(tracers):
            src = pl.multiple_of((t * levels + level) * 8, 8)
            out_ref[pl.ds(src, 8), :] = load(pre, src) + (m0 * new[t][0] + m1 * new[t][1])
        return 0

    lax.fori_loop(0, levels, body, 0, unroll=True)


def swap(x, axis, odd):
    n = lax.axis_size(axis)
    pairs = []
    for i in range(n // 2):
        left = (2 * i + odd) % n
        right = (left + 1) % n
        pairs += [(left, right), (right, left)]
    return lax.ppermute(x, axis, pairs)


def per_device(
    tracers, zonal_velocity, meridional_velocity, diffusivity, land_sea, mix_class, mix_matrices,
    atmos_fluxes, remap_weights, dest_tiles, dest_offsets,
):
    count, levels, lats, lons = tracers.shape
    n_oy, n_ox = lax.axis_size("oy"), lax.axis_size("ox")
    pools = n_oy * n_ox
    oy, ox, sec = lax.axis_index("oy"), lax.axis_index("ox"), lax.axis_index("sec")
    sc = jnp.stack([oy, ox, sec, jnp.int32(n_oy)]).astype(jnp.int32)
    fluxes, atm_rows, _ = atmos_fluxes.shape
    dests = dest_tiles.shape[2]

    dest_t = dest_tiles.transpose(0, 2, 1)
    offset_t = dest_offsets.transpose(0, 2, 1)
    own = lax.dynamic_slice(
        dest_t, (ox, ox * 0, (sec * n_oy + oy) * atm_rows), (1, dests, atm_rows)
    ).reshape(dests, atm_rows)

    def own_section(table):
        part = lax.dynamic_slice(
            table, (ox * 0, ox * 0, sec * (n_oy * atm_rows)), (n_ox, dests, n_oy * atm_rows)
        )
        part = part.reshape(n_ox, dests, n_oy, atm_rows).transpose(2, 0, 3, 1)
        return part.reshape(pools, atm_rows * dests)

    onehot = call(table_kernel, shape(16, pools * 4), [SM, VM, VM])(
        sc, own_section(dest_t), own_section(offset_t)
    )

    tr = tracers.reshape(count * levels * lats, lons)
    u = zonal_velocity.reshape(levels * lats, lons)
    v = meridional_velocity.reshape(levels * lats, lons)
    k = diffusivity.reshape(levels * lats, lons)
    rows = count * levels + 136
    field_specs = half_specs(tr.shape[0]) + half_specs(u.shape[0]) * 3
    edge = 8 * (count + 3)
    nsa, nsb, ewa, ewb = call(
        pack_kernel,
        (shape(rows, lons), shape(rows, lons), shape(edge, 128), shape(edge, 128)),
        [SM] + field_specs + [VM],
    )(sc, tr, tr, u, u, v, v, k, k, land_sea)
    nsa_in, nsb_in = swap(nsa, "oy", 0), swap(nsb, "oy", 1)
    ewa_in, ewb_in = swap(ewa, "ox", 0), swap(ewb, "ox", 1)

    blocks = remap(own, atmos_fluxes, remap_weights[0], pools)
    routed = lax.all_to_all(
        blocks.reshape(pools, 4 * fluxes, 128), ("oy", "ox"), split_axis=0, concat_axis=0, tiled=True
    )

    moved, coef, nsa, nsb, ewa, ewb = call(
        step_one_kernel,
        (
            shape(2, tr.shape[0], 128), shape(5, 2, levels * lats, 128),
            shape(count * levels, lons), shape(count * levels, lons),
            shape(8 * count, 128), shape(8 * count, 128),
        ),
        [SM] + field_specs + [VM] * 7,
        [
            pltpu.VMEM((rows, lons), F32), pltpu.VMEM((rows, lons), F32),
            pltpu.VMEM((2, 64, lons), F32), pltpu.VMEM((2, 64, lons), F32),
        ],
    )(sc, tr, tr, u, u, v, v, k, k, land_sea, nsa_in, nsb_in, ewa_in, ewb_in, ewa, ewb)
    nsa_in, nsb_in = swap(nsa, "oy", 0), swap(nsb, "oy", 1)
    ewa_in, ewb_in = swap(ewa, "ox", 0), swap(ewb, "ox", 1)

    classes = mix_matrices.shape[0]
    top_mats = jnp.pad(mix_matrices[:, :, :2].transpose(2, 1, 0), ((0, 0), (0, 64 - levels), (0, 0)))
    top_mats = top_mats.reshape(128, classes)
    pre, units, top = call(
        step_two_kernel,
        (shape(2, tr.shape[0], 128), shape(2, 2, levels * lats, 128), shape(16 * count, lons)),
        [SM] + [VM] * 9,
        [
            pltpu.VMEM((count * levels, lons), F32), pltpu.VMEM((count * levels, lons), F32),
            pltpu.VMEM((2, count * 512, 128), F32), pltpu.VMEM((64 * classes, 192), BF16),
        ],
    )(sc, moved, coef, nsa_in, nsb_in, ewa_in, ewb_in, mix_matrices, top_mats, mix_class)

    mine = call(combine_kernel, shape(fluxes, lats, lons), [VM, VM])(
        onehot, routed.reshape(pools * 4 * fluxes, 128)
    )
    other = swap(mine, "sec", 0)
    out, surface = call(
        finish_kernel, (shape(*tr.shape), shape(fluxes, lats, lons)), [SM] + [VM] * 6
    )(sc, mine, other, land_sea, top, units, pre)
    return out.reshape(tracers.shape), surface


def solution(mesh):
    placed = (
        P("sec", None, "oy", "ox"),
        P(None, "oy", "ox"),
        P(None, "oy", "ox"),
        P(None, "oy", "ox"),
        P("oy", "ox"),
        P("oy", "ox"),
        P(),
        P(None, ("sec", "oy"), "ox"),
        P("ox", ("sec", "oy"), None, None, None),
        P(),
        P(),
    )
    return jax.shard_map(
        per_device,
        mesh=mesh,
        in_specs=placed,
        out_specs=(P("sec", None, "oy", "ox"), P(None, "oy", "ox")),
        check_vma=False,
    )
```

```python
import jax
import jax.numpy as jnp
from jax import lax
from jax.experimental import pallas as pl
from jax.experimental.pallas import tpu as pltpu
from jax.sharding import PartitionSpec as P

F32 = jnp.float32
BF16 = jnp.bfloat16
MIB = 1024 * 1024
VM = pl.BlockSpec(memory_space=pltpu.VMEM)
SM = pl.BlockSpec(memory_space=pltpu.SMEM)
HB = pl.BlockSpec(memory_space=pltpu.HBM)
OY, OX, SEC, N_OY = 0, 1, 2, 3
UNROLL_ONE = 4
UNROLL_TWO = True
UNROLL_MIX = 4


def call(body, outs, in_specs, scratch=(), out_specs=None, limit=4):
    return pl.pallas_call(
        body,
        out_shape=outs,
        in_specs=in_specs,
        out_specs=out_specs or jax.tree.map(lambda _: VM, outs),
        scratch_shapes=list(scratch),
        compiler_params=pltpu.CompilerParams(vmem_limit_bytes=limit * MIB),
    )


def shape(*dims, dtype=F32):
    return jax.ShapeDtypeStruct(dims, dtype)


def to_tiles(x):
    lats, lons = x.shape[-2:]
    x = x.reshape(-1, lats, 2, lons // 2).transpose(0, 2, 1, 3)
    return x.reshape(-1, lons // 2)


def from_tiles(x, dims):
    x = x.reshape(-1, 2, dims[-2], x.shape[1]).transpose(0, 2, 1, 3)
    return x.reshape(dims)


def tile(ref, n):
    at = pl.multiple_of(n * 16, 16)
    return ref[pl.ds(at, 8), :], ref[pl.ds(at + 8, 8), :]


def put(ref, n, value):
    at = pl.multiple_of(n * 16, 16)
    ref[pl.ds(at, 8), :] = value[0]
    ref[pl.ds(at + 8, 8), :] = value[1]


def latitude(ref, row, count, first=0):
    return tuple(ref[pl.ds(first * 16 + h * 8 + row, count, stride=16), :] for h in range(2))


def one_row(ref, n):
    return ref[0, pl.ds(n, 1), :], ref[1, pl.ds(n, 1), :]


def fetch(pairs, sems):
    copies = [pltpu.make_async_copy(src, dst, sems.at[n]) for n, (src, dst) in enumerate(pairs)]
    for copy in copies:
        copy.start()
    return copies


def field_scratch(tr, u):
    return [pltpu.VMEM(tr.shape, F32)] + [pltpu.VMEM(u.shape, F32)] * 3 + [
        pltpu.VMEM((16, 128), jnp.int32), pltpu.SemaphoreType.DMA((12,))
    ]


def in_place(x):
    return pltpu.with_memory_space_constraint(x, pltpu.HBM)


def fetch_fields(hbm, vmem, sems):
    tr_hbm, tr_ref = hbm[0], vmem[0]
    rows = vmem[1].shape[0]
    cut = rows // 32 * 16
    parts = [
        pl.ds(at + first, size)
        for first, size in ((0, cut), (cut, rows - cut))
        for at in range(0, tr_ref.shape[0], rows)
    ]
    return fetch(
        list(zip(hbm[1:], vmem[1:])) + [(tr_hbm.at[part], tr_ref.at[part]) for part in parts], sems
    )


def remap_kernel(slot_ref, flux_ref, weight_hbm, out_ref, rows_ref, weight_ref, sems):
    fluxes, atm_rows, cells = flux_ref.shape
    dests = weight_ref.shape[1]
    chunks = sems.shape[0]
    size = atm_rows // chunks
    pieces = [pl.ds(n * size, size) for n in range(chunks)]
    copies = fetch([(weight_hbm.at[piece], weight_ref.at[piece]) for piece in pieces], sems)
    rows_ref[...] = flux_ref[...].astype(F32).reshape(fluxes * atm_rows, cells)
    out_ref[...] = jnp.zeros_like(out_ref)
    nothing = jnp.zeros((fluxes, cells), F32)
    for row in range(0, atm_rows, 2):
        if row % size == 0:
            copies[row // size].wait()
        one, two = (rows_ref[pl.ds(r, fluxes, stride=atm_rows), :] for r in (row, row + 1))
        lhs = jnp.concatenate(
            [jnp.concatenate([one, nothing], axis=1), jnp.concatenate([nothing, two], axis=1)], axis=0
        ).astype(BF16)
        for j in range(0, dests, 2):
            rhs = jnp.concatenate(
                [
                    jnp.concatenate([weight_ref[r, j], weight_ref[r, j + 1]], axis=1)
                    for r in (row, row + 1)
                ],
                axis=0,
            )
            parts = jnp.dot(lhs, rhs, preferred_element_type=F32)
            for r in range(2):
                for c in range(2):
                    out_ref[slot_ref[j + c, row + r]] = parts[r * fluxes : r * fluxes + fluxes, c * 128 : c * 128 + 128]


def table_kernel(sc_ref, dest_ref, offset_ref, out_ref):
    lons, dests, _ = dest_ref.shape
    lats = sc_ref[N_OY]
    pool = sc_ref[OY] * lons + sc_ref[OX]
    pools = out_ref.shape[1] // 4
    rows = lons * dests
    low = sc_ref[SEC] == 0
    dest = jnp.concatenate([dest_ref[q] for q in range(lons)], axis=0)
    offset = jnp.concatenate([offset_ref[q] for q in range(lons)], axis=0)
    width = dest.shape[1] // 2
    dest = jnp.where(low, dest[:, :width], dest[:, width:])
    offset = jnp.where(low, offset[:, :width], offset[:, width:])
    group = width // (pools // lons)

    def iota(dims, dim):
        return lax.broadcasted_iota(jnp.int32, dims, dim)

    def flag(x):
        return jnp.where(x, 1.0, 0.0).astype(BF16)

    square = (width, width)
    before = flag(
        (iota(square, 0) // group == iota(square, 1) // group) & (iota(square, 0) < iota(square, 1))
    )
    same_lon = flag(iota((rows, rows), 0) // dests == iota((rows, rows), 1) // dests)
    gather = (width, 128)
    spread = iota(gather, 0) // group == (iota(gather, 1) % pools) // lons
    spread = [flag(spread & (iota(gather, 1) // pools == r)) for r in range(2)]
    keep = iota((rows, 128), 0) // dests == iota((rows, 128), 1) % lons
    for s in range(2):
        hit = dest == pool + s * pools
        rank = jnp.dot(flag(hit), before, preferred_element_type=F32)
        rank = jnp.dot(same_lon, rank.astype(BF16), preferred_element_type=F32)
        place = ((offset & 1) * 8 + s * 4 + (offset >> 1) + 1).astype(F32)
        found = sum(
            jnp.dot(
                jnp.where(hit & (rank == float(r)), place, 0.0).astype(BF16), spread[r],
                preferred_element_type=F32,
            )
            for r in range(2)
        )
        found = jnp.sum(jnp.where(keep, found, 0.0), axis=0, keepdims=True)
        wanted = (iota((16, 128), 0) + 1).astype(F32)
        out_ref[:, s * 128 : s * 128 + 128] = jnp.where(found == wanted, 1.0, 0.0)


def combine_kernel(onehot_ref, recv_ref, after_ref, out_ref):
    fluxes = out_ref.shape[0] // 16
    slots = onehot_ref.shape[1]
    sources = slots // 4
    onehot = onehot_ref[...].astype(BF16)
    for f in range(fluxes):
        cells = jnp.concatenate(
            [recv_ref[pl.ds(n * fluxes + f, sources, stride=4 * fluxes), :] for n in range(4)],
            axis=0,
        )
        high = cells.astype(BF16)
        rest = cells - high.astype(F32)
        mid = rest.astype(BF16)
        low = (rest - mid.astype(F32)).astype(BF16)
        both = jnp.dot(
            onehot, jnp.concatenate([high, mid], axis=1), preferred_element_type=F32
        )
        out_ref[f * 16 : f * 16 + 16, :] = both[:, :128] + (
            both[:, 128:] + jnp.dot(onehot, low, preferred_element_type=F32)
        )


def pack_columns(fields, levels):
    lane = lax.broadcasted_iota(jnp.int32, (8, 128), 1)
    accs = [jnp.zeros((8, 128), F32) for _ in fields]
    for level in range(levels):
        west, east = lane == 2 * level, lane == 2 * level + 1
        for n, (ref, base) in enumerate(fields):
            first, last = tile(ref, base + level)
            acc = jnp.where(west, pltpu.roll(first, 2 * level, 1), accs[n])
            accs[n] = jnp.where(east, pltpu.roll(last, (2 * level + 2) % 128, 1), acc)
    return accs


def select_pair(even, x, y):
    return tuple(jnp.where(even, a, b) for a, b in zip(x, y))


def send_rows(even, north, south, ref_a, ref_b, at, count):
    for h in range(2):
        ref_a[h, at : at + count, :] = jnp.where(even, north[h], south[h])
        ref_b[h, at : at + count, :] = jnp.where(even, south[h], north[h])


def own_slots(sc_ref, dest_hbm, own_ref, sem):
    lons, dests, _ = dest_hbm.shape
    lats = sc_ref[N_OY]
    group = 32
    at = (sc_ref[SEC] * lats + sc_ref[OY]) * group
    aligned = pl.multiple_of(at // 128 * 128, 128)
    copy = pltpu.make_async_copy(dest_hbm.at[sc_ref[OX], :, pl.ds(aligned, 128)], own_ref, sem)
    copy.start()
    copy.wait()
    own = own_ref[...]
    own = jnp.concatenate([own, own], axis=0)
    own = pltpu.roll(own, (128 - (at - aligned)) % 128, 1)
    lane = lax.broadcasted_iota(jnp.int32, own.shape, 1)
    others = [own if n == 0 else pltpu.roll(own, n, 0) for n in range(dests)]
    again = jnp.zeros(own.shape, jnp.int32)
    for back in range(1, group):
        for other in others:
            again = jnp.where((own == pltpu.roll(other, back, 1)) & (lane >= back), 1, again)
    pools = lats * lons
    upper = jnp.where(own >= pools, 1, 0)
    return ((own - upper * pools) * 4 + upper * 2 + again)[:dests]


def pack_kernel(
    sc_ref, tr_hbm, u_hbm, v_hbm, k_hbm, land_hbm, dest_hbm, nsa_ref, nsb_ref, ew_ref, slot_ref,
    tr_ref, u_ref, v_ref, k_ref, land_ref, sems, own_ref, own_sem,
):
    copies = fetch_fields(
        (tr_hbm, u_hbm, v_hbm, k_hbm, land_hbm), (tr_ref, u_ref, v_ref, k_ref, land_ref), sems
    )
    levels = u_ref.shape[0] // 16
    tracers = tr_ref.shape[0] // u_ref.shape[0]
    count = tracers * levels
    even_y = sc_ref[OY] % 2 == 0
    v_at, k_at, w_at = count, count + 64, count + 128
    slot_ref[...] = own_slots(sc_ref, dest_hbm, own_ref, own_sem)
    for copy in copies[:4]:
        copy.wait()
    wet = tuple(x.astype(F32) for x in tile(land_ref, 0))
    for ref, n, at in ((v_ref, levels, v_at), (k_ref, levels, k_at)):
        send_rows(even_y, latitude(ref, 7, n), latitude(ref, 0, n), nsa_ref, nsb_ref, at, n)
    north = tuple(jnp.broadcast_to(x[7:8], x.shape) for x in wet)
    south = tuple(jnp.broadcast_to(x[0:1], x.shape) for x in wet)
    send_rows(even_y, north, south, nsa_ref, nsb_ref, w_at, 8)
    nothing = (jnp.zeros((64 - levels, 128), F32),) * 2
    for at in (v_at + levels, k_at + levels):
        send_rows(even_y, nothing, nothing, nsa_ref, nsb_ref, at, 64 - levels)

    for n, x in enumerate(pack_columns([(u_ref, 0), (k_ref, 0)], levels)):
        ew_ref[(tracers + n) * 8 : (tracers + n) * 8 + 8, :] = x
    for copy in copies[4:]:
        copy.wait()
    send_rows(even_y, latitude(tr_ref, 7, count), latitude(tr_ref, 0, count), nsa_ref, nsb_ref, 0, count)
    for n, x in enumerate(pack_columns([(tr_ref, t * levels) for t in range(tracers)], levels)):
        ew_ref[n * 8 : n * 8 + 8, :] = x
    odd = lax.broadcasted_iota(jnp.int32, (8, 128), 1) % 2 == 1
    ew_ref[(tracers + 2) * 8 :, :] = jnp.where(odd, wet[1][:, 127:], wet[0][:, :1])


def east_of(x, rim):
    lane = lax.broadcasted_iota(jnp.int32, (8, 128), 1)
    first, last = (pltpu.roll(half, 127, 1) for half in x)
    return jnp.where(lane == 127, last, first), jnp.where(lane == 127, rim, last)


def west_of(x, rim):
    lane = lax.broadcasted_iota(jnp.int32, (8, 128), 1)
    first, last = (pltpu.roll(half, 1, 1) for half in x)
    return jnp.where(lane == 0, rim, first), jnp.where(lane == 0, first, last)


def north_of(x, rim):
    row = lax.broadcasted_iota(jnp.int32, (8, 128), 0)
    return tuple(jnp.where(row == 7, r, pltpu.roll(half, 7, 0)) for half, r in zip(x, rim))


def south_of(x, rim):
    row = lax.broadcasted_iota(jnp.int32, (8, 128), 0)
    return tuple(jnp.where(row == 0, r, pltpu.roll(half, 1, 0)) for half, r in zip(x, rim))


def to_ends(rim, level):
    return pltpu.roll(rim, 127 - 2 * level, 1)


def face(vel_left, vel_right, dif_left, dif_right, ww):
    velocity = 0.5 * (vel_left + vel_right)
    spread = 0.5 * (dif_left + dif_right)
    return (
        ww * (jnp.maximum(velocity, 0.0) + spread),
        ww * (jnp.minimum(velocity, 0.0) - spread),
    )


def stencil(coefs, x, rim, north, south):
    middle, ce, cw, cn, cs = coefs
    e, w, n, s = east_of(x, rim), west_of(x, rim), north_of(x, north), south_of(x, south)
    return tuple(
        (middle[h] * x[h] + (ce[h] * e[h] + cw[h] * w[h])) + (cn[h] * n[h] + cs[h] * s[h])
        for h in range(2)
    )


def merge_columns(sc_ref, ewa_ref, ewb_ref):
    even = sc_ref[OX] % 2 == 0
    a, b = ewa_ref[...], ewb_ref[...]
    first = lax.broadcasted_iota(jnp.int32, a.shape, 1) % 2 == 0
    return jnp.where(first, jnp.where(even, a, b), jnp.where(even, b, a))


def merge_rows(sc_ref, nsa_ref, nsb_ref, north_ref, south_ref):
    even = sc_ref[OY] % 2 == 0
    for h in range(2):
        a, b = nsa_ref[h], nsb_ref[h]
        north_ref[h] = jnp.where(even, a, b)
        south_ref[h] = jnp.where(even, b, a)


def step_one_kernel(
    sc_ref, tr_hbm, u_hbm, v_hbm, k_hbm, land_hbm, nsa_hbm, nsb_hbm, ewa_hbm, ewb_hbm, own_hbm,
    new_hbm, coef_hbm, nsa_out, nsb_out, ew_out,
    north_ref, south_ref, face_ref, tr_ref, u_ref, v_ref, k_ref, land_ref, sems,
    nsa_ref, nsb_ref, ewa_ref, ewb_ref, own_ref, rim_sems, new_ref, coef_ref, out_sems,
):
    rim_copies = fetch(
        (
            (nsa_hbm, nsa_ref), (nsb_hbm, nsb_ref), (ewa_hbm, ewa_ref), (ewb_hbm, ewb_ref),
            (own_hbm, own_ref),
        ),
        rim_sems,
    )
    copies = fetch_fields(
        (tr_hbm, u_hbm, v_hbm, k_hbm, land_hbm), (tr_ref, u_ref, v_ref, k_ref, land_ref), sems
    )
    levels = u_ref.shape[0] // 16
    tracers = tr_ref.shape[0] // u_ref.shape[0]
    count = tracers * levels
    even_y = sc_ref[OY] % 2 == 0
    keep_north = (sc_ref[OY] < sc_ref[N_OY] - 1).astype(F32)
    keep_south = (sc_ref[OY] > 0).astype(F32)
    v_at, k_at, w_at = count, count + 64, count + 128
    for copy in rim_copies:
        copy.wait()
    merge_rows(sc_ref, nsa_ref, nsb_ref, north_ref, south_ref)
    for copy in copies[:4]:
        copy.wait()
    wet = tuple(x.astype(F32) for x in tile(land_ref, 0))
    for side, (ref, row, keep) in enumerate(((north_ref, 7, keep_north), (south_ref, 0, keep_south))):
        v_own, k_own = latitude(v_ref, row, levels), latitude(k_ref, row, levels)
        for h in range(2):
            pieces = face(
                v_own[h], ref[h, v_at : v_at + levels, :], k_own[h], ref[h, k_at : k_at + levels, :],
                wet[h][row : row + 1] * ref[h, w_at : w_at + 1, :] * keep,
            )
            for n, x in enumerate(pieces):
                face_ref[side * 2 + n, h, :levels, :] = x
    rims = merge_columns(sc_ref, ewa_ref, ewb_ref)
    own = own_ref[8 * tracers :, :]
    first = lax.broadcasted_iota(jnp.int32, own.shape, 1) % 2 == 0
    own = jnp.where(first, pltpu.roll(own, 127, 1), pltpu.roll(own, 1, 1))
    rim_u, rim_k, rim_w = (rims[8 * (tracers + n) : 8 * (tracers + n + 1)] for n in range(3))
    side_a, side_b = face(own[:8], rim_u, own[8:16], rim_k, own[16:] * rim_w)

    nothing = jnp.zeros((8, 128), F32)
    ww_east = tuple(w * e for w, e in zip(wet, east_of(wet, nothing)))
    ww_north = tuple(w * n for w, n in zip(wet, north_of(wet, (nothing, nothing))))
    last_lane = lax.broadcasted_iota(jnp.int32, (8, 128), 1) == 127
    top_row = lax.broadcasted_iota(jnp.int32, (8, 128), 0) == 7

    def body(level, _):
        ul, vl, kl = tile(u_ref, level), tile(v_ref, level), tile(k_ref, level)
        ue, ke = east_of(ul, nothing), east_of(kl, nothing)
        vn = tuple(pltpu.roll(half, 7, 0) for half in vl)
        kn = tuple(pltpu.roll(half, 7, 0) for half in kl)
        ae, be = zip(*(face(ul[h], ue[h], kl[h], ke[h], ww_east[h]) for h in range(2)))
        an, bn = zip(*(face(vl[h], vn[h], kl[h], kn[h], ww_north[h]) for h in range(2)))
        ends_a, ends_b = to_ends(side_a, level), to_ends(side_b, level)
        ae = ae[0], jnp.where(last_lane, ends_a, ae[1])
        be = be[0], jnp.where(last_lane, ends_b, be[1])
        aw, bw = west_of(ae, ends_a), west_of(be, ends_b)
        an = tuple(jnp.where(top_row, r, x) for r, x in zip(one_row(face_ref.at[0], level), an))
        bn = tuple(jnp.where(top_row, r, x) for r, x in zip(one_row(face_ref.at[1], level), bn))
        as_ = south_of(an, one_row(face_ref.at[2], level))
        bs = south_of(bn, one_row(face_ref.at[3], level))
        middle = tuple(((1.0 - ae[h]) + bw[h]) + (bs[h] - an[h]) for h in range(2))
        coefs = middle, tuple(-x for x in be), aw, tuple(-x for x in bn), as_
        for n, x in enumerate(coefs):
            put(coef_ref, level * 5 + n, x)
        for t in range(tracers):
            n = t * levels + level
            put(
                new_ref, n,
                stencil(
                    coefs, tile(tr_ref, n), to_ends(rims[8 * t : 8 * t + 8], level),
                    one_row(north_ref, n), one_row(south_ref, n),
                ),
            )
        return 0

    out = []
    for n, first, last in ((0, 0, levels // 2), (1, levels // 2, levels)):
        for copy in copies[4 + n * tracers : 4 + n * tracers + tracers]:
            copy.wait()
        lax.fori_loop(first, last, body, 0, unroll=UNROLL_ONE)
        pieces = [(coef_ref, coef_hbm, first * 5, last * 5)]
        pieces += [(new_ref, new_hbm, t * levels + first, t * levels + last) for t in range(tracers)]
        for i, (src, dst, a, b) in enumerate(pieces):
            part = pl.ds(a * 16, (b - a) * 16)
            out.append(pltpu.make_async_copy(src.at[part], dst.at[part], out_sems.at[n * len(pieces) + i]))
            out[-1].start()
    for n, x in enumerate(pack_columns([(new_ref, t * levels) for t in range(tracers)], levels)):
        ew_out[n * 8 : n * 8 + 8, :] = x
    send_rows(
        even_y, latitude(new_ref, 7, count), latitude(new_ref, 0, count), nsa_out, nsb_out, 0, count
    )
    for copy in out:
        copy.wait()


def prepare_kernel(mats_ref, class_ref, lhs_ref, unit_ref, rows_ref):
    levels, classes, _ = mats_ref.shape
    rows_ref[:, :levels] = mats_ref[...].reshape(levels * classes, levels)
    lhs_ref[...] = jnp.zeros_like(lhs_ref)
    tops = []
    for k in range(classes):
        m = rows_ref[pl.ds(k, levels, stride=classes), :]
        high = m.astype(BF16)
        low = (m - high.astype(F32)).astype(BF16)
        for n, x in enumerate((high, low, high)):
            lhs_ref[k * 64 : k * 64 + levels, n * 64 : n * 64 + levels] = x[:, :levels]
        tops.append([jnp.broadcast_to(m[:, n : n + 1], (levels, 128)) for n in range(2)])
    for lat in range(8):
        for h in range(2):
            kind = class_ref[h * 8 + lat : h * 8 + lat + 1, :]
            for n in range(2):
                unit = tops[0][n]
                for k in range(1, classes):
                    unit = jnp.where(kind == k, tops[k][n], unit)
                unit_ref[pl.ds(n * levels * 16 + h * 8 + lat, levels, stride=16), :] = unit


def step_two_kernel(
    sc_ref, tr_hbm, coef_hbm, nsa_ref, nsb_ref, ewa_ref, ewb_ref, lhs_ref, class_ref,
    pre_ref, top_ref,
    north_ref, south_ref, cells_ref, tr_ref, coef_ref, sems,
):
    levels = coef_ref.shape[0] // 80
    tracers = tr_ref.shape[0] // (levels * 16)
    parts = (0, levels // 4), (levels // 4, levels)
    pieces = []
    for a, b in parts:
        pieces.append((coef_hbm, coef_ref, a * 5, b * 5))
        pieces += [(tr_hbm, tr_ref, t * levels + a, t * levels + b) for t in range(tracers)]
    copies = fetch(
        [(src.at[pl.ds(a * 16, (b - a) * 16)], dst.at[pl.ds(a * 16, (b - a) * 16)]) for src, dst, a, b in pieces],
        sems,
    )
    classes = lhs_ref.shape[0] // 64
    merge_rows(sc_ref, nsa_ref, nsb_ref, north_ref, south_ref)
    rims = merge_columns(sc_ref, ewa_ref, ewb_ref)

    def body(level, _):
        coefs = [tile(coef_ref, level * 5 + n) for n in range(5)]
        for t in range(tracers):
            n = t * levels + level
            put(
                cells_ref, t * 64 + level,
                stencil(
                    coefs, tile(tr_ref, n), to_ends(rims[8 * t : 8 * t + 8], level),
                    one_row(north_ref, n), one_row(south_ref, n),
                ),
            )
        return 0

    for n, (first, last) in enumerate(parts):
        for copy in copies[n * (tracers + 1) : (n + 1) * (tracers + 1)]:
            copy.wait()
        lax.fori_loop(first, last, body, 0, unroll=UNROLL_TWO)
    for t in range(tracers):
        at = t * 1024
        top_ref[t * 32 : t * 32 + 32, :] = cells_ref[at : at + 32, :]
        cells_ref[at : at + 32, :] = jnp.zeros((32, 128), F32)
        cells_ref[at + levels * 16 : at + 1024, :] = jnp.zeros((1024 - levels * 16, 128), F32)

    def mix(n, _):
        t, lat = n // 8, n % 8
        x = jnp.concatenate(
            [cells_ref[pl.ds(t * 1024 + h * 8 + lat, 64, stride=16), :] for h in range(2)], axis=1
        )
        high = x.astype(BF16)
        low = (x - high.astype(F32)).astype(BF16)
        mixed = jnp.dot(
            lhs_ref[...], jnp.concatenate([high, high, low], axis=0), preferred_element_type=F32
        )
        for h in range(2):
            lanes = slice(h * 128, h * 128 + 128)
            kind = class_ref[pl.ds(h * 8 + lat, 1), :]
            out = mixed[:64, lanes]
            for k in range(1, classes):
                out = jnp.where(kind == k, mixed[k * 64 : k * 64 + 64, lanes], out)
            pre_ref[pl.ds(t * levels * 16 + h * 8 + lat, levels, stride=16), :] = out[:levels]
        return 0

    lax.fori_loop(0, tracers * 8, mix, 0, unroll=UNROLL_MIX)


def finish_kernel(sc_ref, mine_ref, other_ref, land_ref, top_ref, unit_ref, pre_ref, out_ref, surface_ref):
    levels = unit_ref.shape[0] // 32
    tracers = pre_ref.shape[0] // (levels * 16)
    new = [[], []]
    for h in range(2):
        half = pl.ds(h * 8, 8)
        flux = [
            mine_ref[f * 16 + h * 8 : f * 16 + h * 8 + 8] + other_ref[f * 16 + h * 8 : f * 16 + h * 8 + 8]
            for f in range(8)
        ]
        for f in range(8):
            surface_ref[f * 16 + h * 8 : f * 16 + h * 8 + 8, :] = flux[f]
        wet = land_ref[half, :].astype(F32)
        heat = flux[0] + flux[1] + flux[2] + flux[3]
        fresh = flux[5] - flux[4]
        stress = 0.5 * (flux[6] * flux[6] + flux[7] * flux[7])
        weight = wet * 0.5 * stress / (1.0 + stress)
        for t in range(tracers):
            select = ((sc_ref[SEC] == 0) & (t == 0)).astype(F32)
            top = top_ref[t * 32 + h * 8 : t * 32 + h * 8 + 8, :]
            second = top_ref[t * 32 + 16 + h * 8 : t * 32 + 24 + h * 8, :]
            top = top + wet * (0.25 * select * heat + 0.1 * (1.0 - select) * fresh * top)
            new[h].append((top + weight * (second - top), second + weight * (top - second)))
    for level in range(levels):
        m0, m1 = tile(unit_ref, level), tile(unit_ref, levels + level)
        for t in range(tracers):
            x = tile(pre_ref, t * levels + level)
            put(
                out_ref, t * levels + level,
                tuple(x[h] + (m0[h] * new[h][t][0] + m1[h] * new[h][t][1]) for h in range(2)),
            )


def swap(x, axis, odd):
    n = lax.axis_size(axis)
    pairs = []
    for i in range(n // 2):
        left = (2 * i + odd) % n
        right = (left + 1) % n
        pairs += [(left, right), (right, left)]
    return lax.ppermute(x, axis, pairs)


def per_device(
    tracers, zonal_velocity, meridional_velocity, diffusivity, land_sea, mix_class, mix_matrices,
    atmos_fluxes, remap_weights, dest_tiles, dest_offsets,
):
    count, levels, lats, lons = tracers.shape
    n_oy, n_ox = lax.axis_size("oy"), lax.axis_size("ox")
    pools = n_oy * n_ox
    oy, ox, sec = lax.axis_index("oy"), lax.axis_index("ox"), lax.axis_index("sec")
    sc = jnp.stack([oy, ox, sec, jnp.int32(n_oy)]).astype(jnp.int32)
    fluxes, atm_rows, cells = atmos_fluxes.shape
    dests = dest_tiles.shape[2]
    classes = mix_matrices.shape[0]
    tr, u, v, k = (
        to_tiles(x) for x in (tracers, zonal_velocity, meridional_velocity, diffusivity)
    )
    land, kinds = to_tiles(land_sea), to_tiles(mix_class)

    tr, u, v, k, land_hbm, sc = (in_place(x) for x in (tr, u, v, k, land, sc))
    dest_t = dest_tiles.transpose(0, 2, 1)
    offset_t = dest_offsets.transpose(0, 2, 1)
    rows = count * levels + 136
    edge = 8 * (count + 3)
    nsa, nsb, ew, slots = call(
        pack_kernel,
        (shape(2, rows, 128), shape(2, rows, 128), shape(edge, 128), shape(dests, 128, dtype=jnp.int32)),
        [SM] + [HB] * 6,
        field_scratch(tr, u) + [pltpu.VMEM((dests, 128), jnp.int32), pltpu.SemaphoreType.DMA], limit=8,
    )(sc, tr, u, v, k, land_hbm, in_place(dest_t))
    nsa_in, nsb_in = swap(nsa, "oy", 0), swap(nsb, "oy", 1)
    ewa_in, ewb_in = swap(ew, "ox", 0), swap(ew, "ox", 1)

    blocks = call(
        remap_kernel,
        shape(pools * 4, fluxes, 128),
        [SM, VM, HB],
        [
            pltpu.VMEM((fluxes * atm_rows, cells), F32),
            pltpu.VMEM(remap_weights.shape[1:], BF16), pltpu.SemaphoreType.DMA((8,)),
        ],
        limit=8,
    )(slots, atmos_fluxes, in_place(remap_weights[0]))
    blocks, nsa_in, nsb_in, ewa_in, ewb_in = lax.optimization_barrier(
        (blocks, nsa_in, nsb_in, ewa_in, ewb_in)
    )
    routed = lax.all_to_all(
        blocks.reshape(pools, 4 * fluxes, 128), ("oy", "ox"), split_axis=0, concat_axis=0, tiled=True
    )

    onehot = call(table_kernel, shape(16, pools * 4), [SM, VM, VM])(sc, dest_t, offset_t)
    lhs, units = call(
        prepare_kernel,
        (shape(64 * classes, 192, dtype=BF16), shape(2 * levels * 16, 128)),
        [VM, VM],
        [pltpu.VMEM((levels * classes, 128), F32)],
    )(mix_matrices.transpose(1, 0, 2), kinds)

    moved, coef, nsa, nsb, ew = call(
        step_one_kernel,
        (
            shape(*tr.shape), shape(5 * levels * 16, 128),
            shape(2, count * levels, 128), shape(2, count * levels, 128), shape(8 * count, 128),
        ),
        [SM] + [HB] * 10,
        [pltpu.VMEM((2, rows, 128), F32), pltpu.VMEM((2, rows, 128), F32), pltpu.VMEM((4, 2, 64, 128), F32)]
        + field_scratch(tr, u)
        + [pltpu.VMEM((2, rows, 128), F32)] * 2
        + [pltpu.VMEM((edge, 128), F32)] * 3
        + [
            pltpu.SemaphoreType.DMA((5,)), pltpu.VMEM(tr.shape, F32),
            pltpu.VMEM((5 * levels * 16, 128), F32), pltpu.SemaphoreType.DMA((10,)),
        ],
        [HB, HB, VM, VM, VM],
        60,
    )(sc, tr, u, v, k, land_hbm, *(in_place(x) for x in (nsa_in, nsb_in, ewa_in, ewb_in, ew)))
    nsa_in, nsb_in = swap(nsa, "oy", 0), swap(nsb, "oy", 1)
    ewa_in, ewb_in = swap(ew, "ox", 0), swap(ew, "ox", 1)

    routed, ewa_in, ewb_in = lax.optimization_barrier((routed, ewa_in, ewb_in))
    mine = call(combine_kernel, shape(fluxes * 16, 128), [VM] * 3)(
        onehot, routed.reshape(pools * 4 * fluxes, 128), lhs
    )
    pre, top = call(
        step_two_kernel,
        (shape(*tr.shape), shape(32 * count, 128)),
        [SM, HB, HB] + [VM] * 6,
        [
            pltpu.VMEM((2, count * levels, 128), F32), pltpu.VMEM((2, count * levels, 128), F32),
            pltpu.VMEM((count * 1024, 128), F32), pltpu.VMEM(tr.shape, F32),
            pltpu.VMEM(coef.shape, F32), pltpu.SemaphoreType.DMA((10,)),
        ],
        limit=12,
    )(sc, in_place(moved), in_place(coef), nsa_in, nsb_in, ewa_in, ewb_in, lhs, kinds)

    other = swap(mine, "sec", 0)
    out, surface = call(
        finish_kernel, (shape(*tr.shape), shape(fluxes * 16, 128)), [SM] + [VM] * 6
    )(sc, mine, other, land, top, units, pre)
    return from_tiles(out, tracers.shape), from_tiles(surface, (fluxes, lats, lons))


def solution(mesh):
    placed = (
        P("sec", None, "oy", "ox"),
        P(None, "oy", "ox"),
        P(None, "oy", "ox"),
        P(None, "oy", "ox"),
        P("oy", "ox"),
        P("oy", "ox"),
        P(),
        P(None, ("sec", "oy"), "ox"),
        P("ox", ("sec", "oy"), None, None, None),
        P(),
        P(),
    )
    return jax.shard_map(
        per_device,
        mesh=mesh,
        in_specs=placed,
        out_specs=(P("sec", None, "oy", "ox"), P(None, "oy", "ox")),
        check_vma=False,
    )
```

```python
import jax
import jax.numpy as jnp
from jax import lax
from jax.experimental import pallas as pl
from jax.experimental.pallas import tpu as pltpu
from jax.sharding import PartitionSpec as P

F32 = jnp.float32
BF16 = jnp.bfloat16
MIB = 1024 * 1024
VM = pl.BlockSpec(memory_space=pltpu.VMEM)
SM = pl.BlockSpec(memory_space=pltpu.SMEM)
HB = pl.BlockSpec(memory_space=pltpu.HBM)
OY, OX, SEC, N_OY = 0, 1, 2, 3
UNROLL_ONE = 4
UNROLL_TWO = True
UNROLL_MIX = 16


class Place:
    def __getitem__(self, entry):
        if entry == N_OY:
            return jnp.int32(lax.axis_size("oy"))
        return lax.axis_index(("oy", "ox", "sec")[entry])


def located(body):
    return lambda *refs: body(Place(), *refs)


def call(body, outs, in_specs, scratch=(), out_specs=None, limit=4):
    return pl.pallas_call(
        body,
        out_shape=outs,
        in_specs=in_specs,
        out_specs=out_specs or jax.tree.map(lambda _: VM, outs),
        scratch_shapes=list(scratch),
        compiler_params=pltpu.CompilerParams(vmem_limit_bytes=limit * MIB),
    )


def shape(*dims, dtype=F32):
    return jax.ShapeDtypeStruct(dims, dtype)


def to_tiles(x):
    lats, lons = x.shape[-2:]
    x = x.reshape(-1, lats, 2, lons // 2).transpose(0, 2, 1, 3)
    return x.reshape(-1, lons // 2)


def from_tiles(x, dims):
    x = x.reshape(-1, 2, dims[-2], x.shape[1]).transpose(0, 2, 1, 3)
    return x.reshape(dims)


def tile(ref, n):
    at = pl.multiple_of(n * 16, 16)
    return ref[pl.ds(at, 8), :], ref[pl.ds(at + 8, 8), :]


def put(ref, n, value):
    at = pl.multiple_of(n * 16, 16)
    ref[pl.ds(at, 8), :] = value[0]
    ref[pl.ds(at + 8, 8), :] = value[1]


def latitude(ref, row, count, first=0):
    return tuple(ref[pl.ds(first * 16 + h * 8 + row, count, stride=16), :] for h in range(2))


def one_row(ref, n):
    return ref[0, pl.ds(n, 1), :], ref[1, pl.ds(n, 1), :]


def fetch(pairs, sems):
    copies = [pltpu.make_async_copy(src, dst, sems.at[n]) for n, (src, dst) in enumerate(pairs)]
    for copy in copies:
        copy.start()
    return copies


def field_scratch(tr, u):
    return [pltpu.VMEM(tr.shape, F32)] + [pltpu.VMEM(u.shape, F32)] * 3 + [
        pltpu.VMEM((16, 128), jnp.int32), pltpu.SemaphoreType.DMA((12,))
    ]


def in_place(x):
    return pltpu.with_memory_space_constraint(x, pltpu.HBM)


def fetch_fields(hbm, vmem, sems):
    tr_hbm, tr_ref = hbm[0], vmem[0]
    rows = vmem[1].shape[0]
    cut = rows // 32 * 16
    parts = [
        pl.ds(at + first, size)
        for first, size in ((0, cut), (cut, rows - cut))
        for at in range(0, tr_ref.shape[0], rows)
    ]
    return fetch(
        list(zip(hbm[1:], vmem[1:])) + [(tr_hbm.at[part], tr_ref.at[part]) for part in parts], sems
    )


def remap_kernel(slot_ref, flux_ref, weight_hbm, out_ref, rows_ref, weight_ref, sems):
    fluxes, atm_rows, cells = flux_ref.shape
    dests = weight_ref.shape[1]
    chunks = sems.shape[0]
    size = atm_rows // chunks
    pieces = [pl.ds(n * size, size) for n in range(chunks)]
    copies = fetch([(weight_hbm.at[piece], weight_ref.at[piece]) for piece in pieces], sems)
    rows_ref[...] = flux_ref[...].astype(F32).reshape(fluxes * atm_rows, cells)
    out_ref[...] = jnp.zeros_like(out_ref)
    nothing = jnp.zeros((fluxes, cells), F32)
    for row in range(0, atm_rows, 2):
        if row % size == 0:
            copies[row // size].wait()
        one, two = (rows_ref[pl.ds(r, fluxes, stride=atm_rows), :] for r in (row, row + 1))
        lhs = jnp.concatenate(
            [jnp.concatenate([one, nothing], axis=1), jnp.concatenate([nothing, two], axis=1)], axis=0
        ).astype(BF16)
        for j in range(0, dests, 2):
            rhs = jnp.concatenate(
                [
                    jnp.concatenate([weight_ref[r, j], weight_ref[r, j + 1]], axis=1)
                    for r in (row, row + 1)
                ],
                axis=0,
            )
            parts = jnp.dot(lhs, rhs, preferred_element_type=F32)
            for r in range(2):
                for c in range(2):
                    out_ref[slot_ref[j + c, row + r]] = parts[r * fluxes : r * fluxes + fluxes, c * 128 : c * 128 + 128]


def table_kernel(sc_ref, dest_ref, offset_ref, out_ref):
    lons, dests, _ = dest_ref.shape
    lats = sc_ref[N_OY]
    pool = sc_ref[OY] * lons + sc_ref[OX]
    pools = out_ref.shape[1] // 4
    rows = lons * dests
    low = sc_ref[SEC] == 0
    dest = jnp.concatenate([dest_ref[q] for q in range(lons)], axis=0)
    offset = jnp.concatenate([offset_ref[q] for q in range(lons)], axis=0)
    width = dest.shape[1] // 2
    dest = jnp.where(low, dest[:, :width], dest[:, width:])
    offset = jnp.where(low, offset[:, :width], offset[:, width:])
    group = width // (pools // lons)

    def iota(dims, dim):
        return lax.broadcasted_iota(jnp.int32, dims, dim)

    def flag(x):
        return jnp.where(x, 1.0, 0.0).astype(BF16)

    square = (width, width)
    before = flag(
        (iota(square, 0) // group == iota(square, 1) // group) & (iota(square, 0) < iota(square, 1))
    )
    same_lon = flag(iota((rows, rows), 0) // dests == iota((rows, rows), 1) // dests)
    gather = (width, 128)
    spread = iota(gather, 0) // group == (iota(gather, 1) % pools) // lons
    spread = [flag(spread & (iota(gather, 1) // pools == r)) for r in range(2)]
    keep = iota((rows, 128), 0) // dests == iota((rows, 128), 1) % lons
    for s in range(2):
        hit = dest == pool + s * pools
        rank = jnp.dot(flag(hit), before, preferred_element_type=F32)
        rank = jnp.dot(same_lon, rank.astype(BF16), preferred_element_type=F32)
        place = ((offset & 1) * 8 + s * 4 + (offset >> 1) + 1).astype(F32)
        found = sum(
            jnp.dot(
                jnp.where(hit & (rank == float(r)), place, 0.0).astype(BF16), spread[r],
                preferred_element_type=F32,
            )
            for r in range(2)
        )
        found = jnp.sum(jnp.where(keep, found, 0.0), axis=0, keepdims=True)
        wanted = (iota((16, 128), 0) + 1).astype(F32)
        out_ref[:, s * 128 : s * 128 + 128] = jnp.where(found == wanted, 1.0, 0.0)


def combine_kernel(onehot_ref, recv_ref, after_ref, out_ref):
    fluxes = out_ref.shape[0] // 16
    slots = onehot_ref.shape[1]
    sources = slots // 4
    onehot = onehot_ref[...].astype(BF16)
    for f in range(fluxes):
        cells = jnp.concatenate(
            [recv_ref[pl.ds(n * fluxes + f, sources, stride=4 * fluxes), :] for n in range(4)],
            axis=0,
        )
        high = cells.astype(BF16)
        rest = cells - high.astype(F32)
        mid = rest.astype(BF16)
        low = (rest - mid.astype(F32)).astype(BF16)
        both = jnp.dot(
            onehot, jnp.concatenate([high, mid], axis=1), preferred_element_type=F32
        )
        out_ref[f * 16 : f * 16 + 16, :] = both[:, :128] + (
            both[:, 128:] + jnp.dot(onehot, low, preferred_element_type=F32)
        )


def pack_columns(fields, levels):
    lane = lax.broadcasted_iota(jnp.int32, (8, 128), 1)
    accs = [jnp.zeros((8, 128), F32) for _ in fields]
    for level in range(levels):
        west, east = lane == 2 * level, lane == 2 * level + 1
        for n, (ref, base) in enumerate(fields):
            first, last = tile(ref, base + level)
            acc = jnp.where(west, pltpu.roll(first, 2 * level, 1), accs[n])
            accs[n] = jnp.where(east, pltpu.roll(last, (2 * level + 2) % 128, 1), acc)
    return accs


def select_pair(even, x, y):
    return tuple(jnp.where(even, a, b) for a, b in zip(x, y))


def send_rows(even, north, south, ref_a, ref_b, at, count):
    for h in range(2):
        ref_a[h, at : at + count, :] = jnp.where(even, north[h], south[h])
        ref_b[h, at : at + count, :] = jnp.where(even, south[h], north[h])


def own_slots(sc_ref, dest_hbm, own_ref, sem):
    lons, dests, _ = dest_hbm.shape
    lats = sc_ref[N_OY]
    group = 32
    at = (sc_ref[SEC] * lats + sc_ref[OY]) * group
    aligned = pl.multiple_of(at // 128 * 128, 128)
    copy = pltpu.make_async_copy(dest_hbm.at[sc_ref[OX], :, pl.ds(aligned, 128)], own_ref, sem)
    copy.start()
    copy.wait()
    own = own_ref[...]
    own = jnp.concatenate([own, own], axis=0)
    own = pltpu.roll(own, (128 - (at - aligned)) % 128, 1)
    lane = lax.broadcasted_iota(jnp.int32, own.shape, 1)
    others = [own if n == 0 else pltpu.roll(own, n, 0) for n in range(dests)]
    again = jnp.zeros(own.shape, jnp.int32)
    for back in range(1, group):
        for other in others:
            again = jnp.where((own == pltpu.roll(other, back, 1)) & (lane >= back), 1, again)
    pools = lats * lons
    upper = jnp.where(own >= pools, 1, 0)
    return ((own - upper * pools) * 4 + upper * 2 + again)[:dests]


def pack_kernel(
    sc_ref, tr_hbm, u_hbm, v_hbm, k_hbm, land_hbm, dest_hbm, nsa_ref, nsb_ref, ew_ref, slot_ref,
    tr_ref, u_ref, v_ref, k_ref, land_ref, sems, own_ref, own_sem,
):
    copies = fetch_fields(
        (tr_hbm, u_hbm, v_hbm, k_hbm, land_hbm), (tr_ref, u_ref, v_ref, k_ref, land_ref), sems
    )
    levels = u_ref.shape[0] // 16
    tracers = tr_ref.shape[0] // u_ref.shape[0]
    count = tracers * levels
    even_y = sc_ref[OY] % 2 == 0
    v_at, k_at, w_at = count, count + 64, count + 128
    slot_ref[...] = own_slots(sc_ref, dest_hbm, own_ref, own_sem)
    for copy in copies[:4]:
        copy.wait()
    wet = tuple(x.astype(F32) for x in tile(land_ref, 0))
    for ref, n, at in ((v_ref, levels, v_at), (k_ref, levels, k_at)):
        send_rows(even_y, latitude(ref, 7, n), latitude(ref, 0, n), nsa_ref, nsb_ref, at, n)
    north = tuple(jnp.broadcast_to(x[7:8], x.shape) for x in wet)
    south = tuple(jnp.broadcast_to(x[0:1], x.shape) for x in wet)
    send_rows(even_y, north, south, nsa_ref, nsb_ref, w_at, 8)
    nothing = (jnp.zeros((64 - levels, 128), F32),) * 2
    for at in (v_at + levels, k_at + levels):
        send_rows(even_y, nothing, nothing, nsa_ref, nsb_ref, at, 64 - levels)

    for n, x in enumerate(pack_columns([(u_ref, 0), (k_ref, 0)], levels)):
        ew_ref[(tracers + n) * 8 : (tracers + n) * 8 + 8, :] = x
    for copy in copies[4:]:
        copy.wait()
    send_rows(even_y, latitude(tr_ref, 7, count), latitude(tr_ref, 0, count), nsa_ref, nsb_ref, 0, count)
    for n, x in enumerate(pack_columns([(tr_ref, t * levels) for t in range(tracers)], levels)):
        ew_ref[n * 8 : n * 8 + 8, :] = x
    odd = lax.broadcasted_iota(jnp.int32, (8, 128), 1) % 2 == 1
    ew_ref[(tracers + 2) * 8 :, :] = jnp.where(odd, wet[1][:, 127:], wet[0][:, :1])


def east_of(x, rim):
    lane = lax.broadcasted_iota(jnp.int32, (8, 128), 1)
    first, last = (pltpu.roll(half, 127, 1) for half in x)
    return jnp.where(lane == 127, last, first), jnp.where(lane == 127, rim, last)


def west_of(x, rim):
    lane = lax.broadcasted_iota(jnp.int32, (8, 128), 1)
    first, last = (pltpu.roll(half, 1, 1) for half in x)
    return jnp.where(lane == 0, rim, first), jnp.where(lane == 0, first, last)


def north_of(x, rim):
    row = lax.broadcasted_iota(jnp.int32, (8, 128), 0)
    return tuple(jnp.where(row == 7, r, pltpu.roll(half, 7, 0)) for half, r in zip(x, rim))


def south_of(x, rim):
    row = lax.broadcasted_iota(jnp.int32, (8, 128), 0)
    return tuple(jnp.where(row == 0, r, pltpu.roll(half, 1, 0)) for half, r in zip(x, rim))


def to_ends(rim, level):
    return pltpu.roll(rim, 127 - 2 * level, 1)


def face(vel_left, vel_right, dif_left, dif_right, ww):
    velocity = 0.5 * (vel_left + vel_right)
    spread = 0.5 * (dif_left + dif_right)
    return (
        ww * (jnp.maximum(velocity, 0.0) + spread),
        ww * (jnp.minimum(velocity, 0.0) - spread),
    )


def stencil(coefs, x, rim, north, south):
    middle, ce, cw, cn, cs = coefs
    e, w, n, s = east_of(x, rim), west_of(x, rim), north_of(x, north), south_of(x, south)
    return tuple(
        (middle[h] * x[h] + (ce[h] * e[h] + cw[h] * w[h])) + (cn[h] * n[h] + cs[h] * s[h])
        for h in range(2)
    )


def merge_columns(sc_ref, ewa_ref, ewb_ref):
    even = sc_ref[OX] % 2 == 0
    a, b = ewa_ref[...], ewb_ref[...]
    first = lax.broadcasted_iota(jnp.int32, a.shape, 1) % 2 == 0
    return jnp.where(first, jnp.where(even, a, b), jnp.where(even, b, a))


def merge_rows(sc_ref, nsa_ref, nsb_ref, north_ref, south_ref):
    even = sc_ref[OY] % 2 == 0
    for h in range(2):
        a, b = nsa_ref[h], nsb_ref[h]
        north_ref[h] = jnp.where(even, a, b)
        south_ref[h] = jnp.where(even, b, a)


def step_one_kernel(
    sc_ref, tr_hbm, u_hbm, v_hbm, k_hbm, land_hbm, nsa_hbm, nsb_hbm, ewa_hbm, ewb_hbm, own_hbm,
    new_hbm, coef_hbm, nsa_out, nsb_out, ew_out,
    north_ref, south_ref, face_ref, tr_ref, u_ref, v_ref, k_ref, land_ref, sems,
    nsa_ref, nsb_ref, ewa_ref, ewb_ref, own_ref, rim_sems, new_ref, coef_ref, out_sems,
):
    rim_copies = fetch(
        (
            (nsa_hbm, nsa_ref), (nsb_hbm, nsb_ref), (ewa_hbm, ewa_ref), (ewb_hbm, ewb_ref),
            (own_hbm, own_ref),
        ),
        rim_sems,
    )
    copies = fetch_fields(
        (tr_hbm, u_hbm, v_hbm, k_hbm, land_hbm), (tr_ref, u_ref, v_ref, k_ref, land_ref), sems
    )
    levels = u_ref.shape[0] // 16
    tracers = tr_ref.shape[0] // u_ref.shape[0]
    count = tracers * levels
    even_y = sc_ref[OY] % 2 == 0
    keep_north = (sc_ref[OY] < sc_ref[N_OY] - 1).astype(F32)
    keep_south = (sc_ref[OY] > 0).astype(F32)
    v_at, k_at, w_at = count, count + 64, count + 128
    for copy in rim_copies:
        copy.wait()
    merge_rows(sc_ref, nsa_ref, nsb_ref, north_ref, south_ref)
    for copy in copies[:4]:
        copy.wait()
    wet = tuple(x.astype(F32) for x in tile(land_ref, 0))
    for side, (ref, row, keep) in enumerate(((north_ref, 7, keep_north), (south_ref, 0, keep_south))):
        v_own, k_own = latitude(v_ref, row, levels), latitude(k_ref, row, levels)
        for h in range(2):
            pieces = face(
                v_own[h], ref[h, v_at : v_at + levels, :], k_own[h], ref[h, k_at : k_at + levels, :],
                wet[h][row : row + 1] * ref[h, w_at : w_at + 1, :] * keep,
            )
            for n, x in enumerate(pieces):
                face_ref[side * 2 + n, h, :levels, :] = x
    rims = merge_columns(sc_ref, ewa_ref, ewb_ref)
    own = own_ref[8 * tracers :, :]
    first = lax.broadcasted_iota(jnp.int32, own.shape, 1) % 2 == 0
    own = jnp.where(first, pltpu.roll(own, 127, 1), pltpu.roll(own, 1, 1))
    rim_u, rim_k, rim_w = (rims[8 * (tracers + n) : 8 * (tracers + n + 1)] for n in range(3))
    side_a, side_b = face(own[:8], rim_u, own[8:16], rim_k, own[16:] * rim_w)

    nothing = jnp.zeros((8, 128), F32)
    ww_east = tuple(w * e for w, e in zip(wet, east_of(wet, nothing)))
    ww_north = tuple(w * n for w, n in zip(wet, north_of(wet, (nothing, nothing))))
    last_lane = lax.broadcasted_iota(jnp.int32, (8, 128), 1) == 127
    top_row = lax.broadcasted_iota(jnp.int32, (8, 128), 0) == 7

    def body(level, _):
        ul, vl, kl = tile(u_ref, level), tile(v_ref, level), tile(k_ref, level)
        ue, ke = east_of(ul, nothing), east_of(kl, nothing)
        vn = tuple(pltpu.roll(half, 7, 0) for half in vl)
        kn = tuple(pltpu.roll(half, 7, 0) for half in kl)
        ae, be = zip(*(face(ul[h], ue[h], kl[h], ke[h], ww_east[h]) for h in range(2)))
        an, bn = zip(*(face(vl[h], vn[h], kl[h], kn[h], ww_north[h]) for h in range(2)))
        ends_a, ends_b = to_ends(side_a, level), to_ends(side_b, level)
        ae = ae[0], jnp.where(last_lane, ends_a, ae[1])
        be = be[0], jnp.where(last_lane, ends_b, be[1])
        aw, bw = west_of(ae, ends_a), west_of(be, ends_b)
        an = tuple(jnp.where(top_row, r, x) for r, x in zip(one_row(face_ref.at[0], level), an))
        bn = tuple(jnp.where(top_row, r, x) for r, x in zip(one_row(face_ref.at[1], level), bn))
        as_ = south_of(an, one_row(face_ref.at[2], level))
        bs = south_of(bn, one_row(face_ref.at[3], level))
        middle = tuple(((1.0 - ae[h]) + bw[h]) + (bs[h] - an[h]) for h in range(2))
        coefs = middle, tuple(-x for x in be), aw, tuple(-x for x in bn), as_
        for n, x in enumerate(coefs):
            put(coef_ref, level * 5 + n, x)
        for t in range(tracers):
            n = t * levels + level
            put(
                new_ref, n,
                stencil(
                    coefs, tile(tr_ref, n), to_ends(rims[8 * t : 8 * t + 8], level),
                    one_row(north_ref, n), one_row(south_ref, n),
                ),
            )
        return 0

    out = []
    for n, first, last in ((0, 0, levels // 2), (1, levels // 2, levels)):
        for copy in copies[4 + n * tracers : 4 + n * tracers + tracers]:
            copy.wait()
        lax.fori_loop(first, last, body, 0, unroll=UNROLL_ONE)
        pieces = [(coef_ref, coef_hbm, first * 5, last * 5)]
        pieces += [(new_ref, new_hbm, t * levels + first, t * levels + last) for t in range(tracers)]
        for i, (src, dst, a, b) in enumerate(pieces):
            part = pl.ds(a * 16, (b - a) * 16)
            out.append(pltpu.make_async_copy(src.at[part], dst.at[part], out_sems.at[n * len(pieces) + i]))
            out[-1].start()
    for n, x in enumerate(pack_columns([(new_ref, t * levels) for t in range(tracers)], levels)):
        ew_out[n * 8 : n * 8 + 8, :] = x
    send_rows(
        even_y, latitude(new_ref, 7, count), latitude(new_ref, 0, count), nsa_out, nsb_out, 0, count
    )
    for copy in out:
        copy.wait()


def prepare_kernel(mats_ref, class_ref, lhs_ref, unit_ref, rows_ref):
    levels, classes, _ = mats_ref.shape
    rows_ref[:, :levels] = mats_ref[...].reshape(levels * classes, levels)
    lhs_ref[...] = jnp.zeros_like(lhs_ref)
    tops = []
    for k in range(classes):
        m = rows_ref[pl.ds(k, levels, stride=classes), :]
        high = m.astype(BF16)
        low = (m - high.astype(F32)).astype(BF16)
        for n, x in enumerate((high, low, high)):
            lhs_ref[k * 64 : k * 64 + levels, n * 64 : n * 64 + levels] = x[:, :levels]
        tops.append([jnp.broadcast_to(m[:, n : n + 1], (levels, 128)) for n in range(2)])
    for lat in range(8):
        for h in range(2):
            kind = class_ref[h * 8 + lat : h * 8 + lat + 1, :]
            for n in range(2):
                unit = tops[0][n]
                for k in range(1, classes):
                    unit = jnp.where(kind == k, tops[k][n], unit)
                unit_ref[pl.ds(n * levels * 16 + h * 8 + lat, levels, stride=16), :] = unit


def step_two_kernel(
    sc_ref, tr_hbm, coef_hbm, nsa_ref, nsb_ref, ewa_ref, ewb_ref, lhs_ref, class_ref,
    pre_ref, top_ref,
    north_ref, south_ref, cells_ref, tr_ref, coef_ref, sems,
):
    levels = coef_ref.shape[0] // 80
    tracers = tr_ref.shape[0] // (levels * 16)
    parts = (0, levels // 4), (levels // 4, levels)
    pieces = []
    for a, b in parts:
        pieces.append((coef_hbm, coef_ref, a * 5, b * 5))
        pieces += [(tr_hbm, tr_ref, t * levels + a, t * levels + b) for t in range(tracers)]
    copies = fetch(
        [(src.at[pl.ds(a * 16, (b - a) * 16)], dst.at[pl.ds(a * 16, (b - a) * 16)]) for src, dst, a, b in pieces],
        sems,
    )
    classes = lhs_ref.shape[0] // 64
    merge_rows(sc_ref, nsa_ref, nsb_ref, north_ref, south_ref)
    rims = merge_columns(sc_ref, ewa_ref, ewb_ref)

    def body(level, _):
        coefs = [tile(coef_ref, level * 5 + n) for n in range(5)]
        for t in range(tracers):
            n = t * levels + level
            put(
                cells_ref, t * 64 + level,
                stencil(
                    coefs, tile(tr_ref, n), to_ends(rims[8 * t : 8 * t + 8], level),
                    one_row(north_ref, n), one_row(south_ref, n),
                ),
            )
        return 0

    for n, (first, last) in enumerate(parts):
        for copy in copies[n * (tracers + 1) : (n + 1) * (tracers + 1)]:
            copy.wait()
        lax.fori_loop(first, last, body, 0, unroll=UNROLL_TWO)
    for t in range(tracers):
        at = t * 1024
        top_ref[t * 32 : t * 32 + 32, :] = cells_ref[at : at + 32, :]
        cells_ref[at : at + 32, :] = jnp.zeros((32, 128), F32)
        cells_ref[at + levels * 16 : at + 1024, :] = jnp.zeros((1024 - levels * 16, 128), F32)

    def mix(n, _):
        t, lat = n // 8, n % 8
        x = jnp.concatenate(
            [cells_ref[pl.ds(t * 1024 + h * 8 + lat, 64, stride=16), :] for h in range(2)], axis=1
        )
        high = x.astype(BF16)
        low = (x - high.astype(F32)).astype(BF16)
        mixed = jnp.dot(
            lhs_ref[...], jnp.concatenate([high, high, low], axis=0), preferred_element_type=F32
        )
        for h in range(2):
            lanes = slice(h * 128, h * 128 + 128)
            kind = class_ref[pl.ds(h * 8 + lat, 1), :]
            out = mixed[:64, lanes]
            for k in range(1, classes):
                out = jnp.where(kind == k, mixed[k * 64 : k * 64 + 64, lanes], out)
            pre_ref[pl.ds(t * levels * 16 + h * 8 + lat, levels, stride=16), :] = out[:levels]
        return 0

    lax.fori_loop(0, tracers * 8, mix, 0, unroll=UNROLL_MIX)


def finish_kernel(sc_ref, mine_ref, other_ref, land_ref, top_ref, unit_ref, pre_ref, out_ref, surface_ref):
    levels = unit_ref.shape[0] // 32
    tracers = pre_ref.shape[0] // (levels * 16)
    new = [[], []]
    for h in range(2):
        half = pl.ds(h * 8, 8)
        flux = [
            mine_ref[f * 16 + h * 8 : f * 16 + h * 8 + 8] + other_ref[f * 16 + h * 8 : f * 16 + h * 8 + 8]
            for f in range(8)
        ]
        for f in range(8):
            surface_ref[f * 16 + h * 8 : f * 16 + h * 8 + 8, :] = flux[f]
        wet = land_ref[half, :].astype(F32)
        heat = flux[0] + flux[1] + flux[2] + flux[3]
        fresh = flux[5] - flux[4]
        stress = 0.5 * (flux[6] * flux[6] + flux[7] * flux[7])
        weight = wet * 0.5 * stress / (1.0 + stress)
        for t in range(tracers):
            select = ((sc_ref[SEC] == 0) & (t == 0)).astype(F32)
            top = top_ref[t * 32 + h * 8 : t * 32 + h * 8 + 8, :]
            second = top_ref[t * 32 + 16 + h * 8 : t * 32 + 24 + h * 8, :]
            top = top + wet * (0.25 * select * heat + 0.1 * (1.0 - select) * fresh * top)
            new[h].append((top + weight * (second - top), second + weight * (top - second)))
    for level in range(levels):
        m0, m1 = tile(unit_ref, level), tile(unit_ref, levels + level)
        for t in range(tracers):
            x = tile(pre_ref, t * levels + level)
            put(
                out_ref, t * levels + level,
                tuple(x[h] + (m0[h] * new[h][t][0] + m1[h] * new[h][t][1]) for h in range(2)),
            )


def swap(x, axis, odd):
    n = lax.axis_size(axis)
    pairs = []
    for i in range(n // 2):
        left = (2 * i + odd) % n
        right = (left + 1) % n
        pairs += [(left, right), (right, left)]
    return lax.ppermute(x, axis, pairs)


def per_device(
    tracers, zonal_velocity, meridional_velocity, diffusivity, land_sea, mix_class, mix_matrices,
    atmos_fluxes, remap_weights, dest_tiles, dest_offsets,
):
    count, levels, lats, lons = tracers.shape
    n_oy, n_ox = lax.axis_size("oy"), lax.axis_size("ox")
    pools = n_oy * n_ox
    fluxes, atm_rows, cells = atmos_fluxes.shape
    dests = dest_tiles.shape[2]
    classes = mix_matrices.shape[0]
    tr, u, v, k = (
        to_tiles(x) for x in (tracers, zonal_velocity, meridional_velocity, diffusivity)
    )
    land, kinds = to_tiles(land_sea), to_tiles(mix_class)

    tr, u, v, k, land_hbm = (in_place(x) for x in (tr, u, v, k, land))
    dest_t = dest_tiles.transpose(0, 2, 1)
    offset_t = dest_offsets.transpose(0, 2, 1)
    rows = count * levels + 136
    edge = 8 * (count + 3)
    nsa, nsb, ew, slots = call(
        located(pack_kernel),
        (shape(2, rows, 128), shape(2, rows, 128), shape(edge, 128), shape(dests, 128, dtype=jnp.int32)),
        [HB] * 6,
        field_scratch(tr, u) + [pltpu.VMEM((dests, 128), jnp.int32), pltpu.SemaphoreType.DMA], limit=8,
    )(tr, u, v, k, land_hbm, in_place(dest_t))
    nsa_in, nsb_in = swap(nsa, "oy", 0), swap(nsb, "oy", 1)
    ewa_in, ewb_in = swap(ew, "ox", 0), swap(ew, "ox", 1)

    blocks = call(
        remap_kernel,
        shape(pools * 4, fluxes, 128),
        [SM, VM, HB],
        [
            pltpu.VMEM((fluxes * atm_rows, cells), F32),
            pltpu.VMEM(remap_weights.shape[1:], BF16), pltpu.SemaphoreType.DMA((8,)),
        ],
        limit=8,
    )(slots, atmos_fluxes, in_place(remap_weights[0]))
    blocks, nsa_in, nsb_in, ewa_in, ewb_in = lax.optimization_barrier(
        (blocks, nsa_in, nsb_in, ewa_in, ewb_in)
    )
    routed = lax.all_to_all(
        blocks.reshape(pools, 4 * fluxes, 128), ("oy", "ox"), split_axis=0, concat_axis=0, tiled=True
    )

    onehot = call(located(table_kernel), shape(16, pools * 4), [VM, VM])(dest_t, offset_t)
    lhs, units = call(
        prepare_kernel,
        (shape(64 * classes, 192, dtype=BF16), shape(2 * levels * 16, 128)),
        [VM, VM],
        [pltpu.VMEM((levels * classes, 128), F32)],
    )(mix_matrices.transpose(1, 0, 2), kinds)

    moved, coef, nsa, nsb, ew = call(
        located(step_one_kernel),
        (
            shape(*tr.shape), shape(5 * levels * 16, 128),
            shape(2, count * levels, 128), shape(2, count * levels, 128), shape(8 * count, 128),
        ),
        [HB] * 10,
        [pltpu.VMEM((2, rows, 128), F32), pltpu.VMEM((2, rows, 128), F32), pltpu.VMEM((4, 2, 64, 128), F32)]
        + field_scratch(tr, u)
        + [pltpu.VMEM((2, rows, 128), F32)] * 2
        + [pltpu.VMEM((edge, 128), F32)] * 3
        + [
            pltpu.SemaphoreType.DMA((5,)), pltpu.VMEM(tr.shape, F32),
            pltpu.VMEM((5 * levels * 16, 128), F32), pltpu.SemaphoreType.DMA((10,)),
        ],
        [HB, HB, VM, VM, VM],
        60,
    )(tr, u, v, k, land_hbm, *(in_place(x) for x in (nsa_in, nsb_in, ewa_in, ewb_in, ew)))
    nsa_in, nsb_in = swap(nsa, "oy", 0), swap(nsb, "oy", 1)
    ewa_in, ewb_in = swap(ew, "ox", 0), swap(ew, "ox", 1)

    routed, ewa_in, ewb_in = lax.optimization_barrier((routed, ewa_in, ewb_in))
    mine = call(combine_kernel, shape(fluxes * 16, 128), [VM] * 3)(
        onehot, routed.reshape(pools * 4 * fluxes, 128), lhs
    )
    pre, top = call(
        located(step_two_kernel),
        (shape(*tr.shape), shape(32 * count, 128)),
        [HB, HB] + [VM] * 6,
        [
            pltpu.VMEM((2, count * levels, 128), F32), pltpu.VMEM((2, count * levels, 128), F32),
            pltpu.VMEM((count * 1024, 128), F32), pltpu.VMEM(tr.shape, F32),
            pltpu.VMEM(coef.shape, F32), pltpu.SemaphoreType.DMA((10,)),
        ],
        limit=12,
    )(in_place(moved), in_place(coef), nsa_in, nsb_in, ewa_in, ewb_in, lhs, kinds)

    other = swap(mine, "sec", 0)
    out, surface = call(
        located(finish_kernel), (shape(*tr.shape), shape(fluxes * 16, 128)), [VM] * 6
    )(mine, other, land, top, units, pre)
    return from_tiles(out, tracers.shape), from_tiles(surface, (fluxes, lats, lons))


def solution(mesh):
    placed = (
        P("sec", None, "oy", "ox"),
        P(None, "oy", "ox"),
        P(None, "oy", "ox"),
        P(None, "oy", "ox"),
        P("oy", "ox"),
        P("oy", "ox"),
        P(),
        P(None, ("sec", "oy"), "ox"),
        P("ox", ("sec", "oy"), None, None, None),
        P(),
        P(),
    )
    return jax.shard_map(
        per_device,
        mesh=mesh,
        in_specs=placed,
        out_specs=(P("sec", None, "oy", "ox"), P(None, "oy", "ox")),
        check_vma=False,
    )
```
